256 devices in a mesh: dom: 64 (over x, z, core), rhs: 4 (over y).
Axes of the slice: x: 4, y: 4, z: 8, core: 2. Of those that a mesh axis runs over, the one named last changes fastest.
Arguments:
- solution: float32 [768, 64, 192], P('dom', 'rhs'), may hold values from -6 to 6
- loads: float32 [768, 64, 192], P('dom', 'rhs'), may hold values from -6 to 6
- blocks: float32 [768, 4, 36864], P('dom'), may hold values from -0.21875 to 0.21875
- columns: int32 [768, 4], P('dom'), may hold values from 0 to 767, as said below
- row_source: int32 [768], P('dom'), may hold values from 0 to 767, each once
- inverses: bfloat16 [512, 36864], P('dom'), may hold values from -0.4375 to 0.4375
- tiles: bfloat16 [512, 8, 36864], P('dom'), may hold values from -0.15625 to 0.15625
- targets: int32 [512, 8], P('dom'), may hold values from 0 to 255, as said below
Outputs:
- level_solution: bfloat16 [512, 64, 192], P('dom', 'rhs')
- ancestor_rhs: float32 [256, 64, 192], P('dom', 'rhs')
- residual_rms: float32 [], replicated
The draws below stay inside these ranges and needn't reach their ends.
Inputs may be any that keep to these rules, and one draw needn't show every extreme that they name: `columns`: for a block row in partition d (rows d * 12 to d * 12 + 11), every column lies in partitions d - 1 to d + 1. `targets`: ancestor block t is held by owner t // 4. Of the 64 tiles of one owner, at most 2 target blocks of any one owner, and one owner receives exactly 2 tiles from every owner.
All inputs are finite; a program needn't handle non-finite values.
Results may differ from the reference program's by a relative error of at most 0.0055.
Values may be sent and summed in bfloat16 or wider, within the bound.
No kernel may reach another device: no remote copies, remote signals or barrier semaphores. Data moves between devices by JAX's collectives and lax.ppermute only.
A program may use at most 128 MiB of HBM per device.

```python
import jax
import jax.numpy as jnp
from jax import lax

B = 192
R = 64
LEAF = 8
ANC = 4
NNZ = 4
UPD = 8
P_SIZE = 12
NBLK = 768
NLEAF = 512
NANC = 256
CAP = 2
N_DOM = 64


def draw_columns(key, part):
    key = jax.random.fold_in(key, 11)
    offsets = jax.random.randint(key, (NBLK, NNZ), 0, 3 * P_SIZE)
    row_partition = (jnp.arange(NBLK, dtype=jnp.int32) // P_SIZE)[:, None]
    global_index = row_partition * P_SIZE - P_SIZE + offsets
    global_index = jnp.where(global_index < 0, global_index + P_SIZE, global_index)
    global_index = jnp.where(global_index >= NBLK, global_index - P_SIZE, global_index)
    return global_index.astype(jnp.int32)


def draw_targets(key, part):
    key = jax.random.fold_in(key, 23)
    key_root, key_owner, key_block = jax.random.split(key, 3)
    tile_count = LEAF * UPD
    root_owner = jax.random.randint(key_root, (), 0, N_DOM)
    ordinals = jnp.arange(tile_count, dtype=jnp.int32)

    def owner_row(sub_key):
        key_other, key_shuffle = jax.random.split(sub_key)
        other_owners = jax.random.permutation(key_other, N_DOM - 1)
        chosen = other_owners[(ordinals - CAP) % (N_DOM - 1)]
        chosen = jnp.where(chosen >= root_owner, chosen + 1, chosen)
        owners_row = jnp.where(ordinals < CAP, root_owner, chosen)
        shuffle = jax.random.permutation(key_shuffle, tile_count)
        return owners_row[shuffle]
    owners = jax.vmap(owner_row)(jax.random.split(key_owner, N_DOM))
    block_index = jax.random.randint(key_block, (N_DOM, tile_count), 0, ANC)
    return (owners * ANC + block_index).reshape(NLEAF, UPD).astype(jnp.int32)


def block_levels(key, shape, cuts, low, high):
    def one(dim, parts):
        heights = jax.random.uniform(jax.random.fold_in(jax.random.fold_in(key, 6), dim), (parts,), jnp.float32, low / len(cuts), high / len(cuts))
        return jnp.repeat(jnp.exp(heights), shape[dim] // parts).reshape((-1,) + (1,) * (len(shape) - dim - 1))

    level = one(*cuts[0])
    for cut in cuts[1:]:
        level = level * one(*cut)
    return level


def noise(stream_key, extent, spread, bound, pieces=(), kind=jnp.bfloat16):
    entries = jax.random.normal(stream_key, extent, jnp.float32) * spread
    if len(pieces) > 0:
        entries = block_levels(stream_key, extent, pieces, -0.22, 0.18) * entries
    return jnp.clip(entries, min=-bound, max=bound).astype(kind)


def setup_inputs(seed: int = 0) -> dict:
    key_list = jax.random.split(jax.random.key(seed), 9)
    solution = noise(key_list[0], (NBLK, R, B), 1.0, 6.0, ((0, 64), (1, 4)), jnp.float32)
    loads = noise(key_list[1], (NBLK, R, B), 1.0, 6.0, ((0, 64), (1, 4)), jnp.float32)
    blocks = noise(key_list[2], (NBLK, NNZ, B * B), (B * NNZ) ** -0.5, 0.21875, ((0, 64),), jnp.float32)
    columns = draw_columns(jax.random.fold_in(key_list[8], 71), 0)
    row_source = jax.random.permutation(key_list[4], NBLK).astype(jnp.int32)
    inverses = noise(key_list[5], (NLEAF, B * B), B ** -0.5, 0.4375, ((0, 64),))
    tiles = noise(key_list[6], (NLEAF, UPD, B * B), (B * UPD) ** -0.5, 0.15625, ((0, 64),))
    targets = draw_targets(jax.random.fold_in(key_list[8], 71), 0)
    return {"solution": solution, "loads": loads, "blocks": blocks, "columns": columns, "row_source": row_source, "inverses": inverses, "tiles": tiles, "targets": targets}


def reference(solution, loads, blocks, columns, row_source, inverses, tiles, targets):
    neighbours = solution[columns]
    square_blocks = blocks.reshape(NBLK, NNZ, B, B)
    products = jnp.einsum('gjae,gjce->gca', square_blocks, neighbours, precision=lax.Precision.HIGHEST)
    residual = loads - products
    residual_rms = jnp.sqrt(jnp.sum(residual * residual) / (NBLK * R * B))
    rounded = residual.astype(jnp.bfloat16)
    relaid = rounded[row_source].reshape(N_DOM, P_SIZE, R, B)
    leaf_rows = relaid[:, :LEAF].reshape(NLEAF, R, B)
    ancestor_rows = relaid[:, LEAF:].reshape(NANC, R, B)
    square_inverses = inverses.reshape(NLEAF, B, B)
    level_solution = jnp.einsum('kae,kce->kca', square_inverses.astype(jnp.float32), leaf_rows.astype(jnp.float32)).astype(jnp.bfloat16)
    square_tiles = tiles.reshape(NLEAF, UPD, B, B)
    updates = jnp.einsum('kmae,kce->kmca', square_tiles.astype(jnp.float32), level_solution.astype(jnp.float32))
    summed = jax.ops.segment_sum(updates.reshape(NLEAF * UPD, R, B), targets.reshape(-1), NANC)
    ancestor_rhs = ancestor_rows.astype(jnp.float32) - summed
    return (level_solution, ancestor_rhs, residual_rms)
```

```python
import jax
import jax.numpy as jnp
from jax import lax
from jax.experimental import pallas as pl
from jax.experimental.pallas import tpu as pltpu
from jax.sharding import PartitionSpec as P

B = 192
LEAF = 8
ANC = 4
NNZ = 4
UPD = 8
P_SIZE = 12
CASES = 16
DOM = 64
N_X, N_Z, N_CORE = 4, 8, 2
GROUP = N_X * N_CORE
LANES = 128
ROWS = 8
PAIRS = B // 2
BF16 = jnp.bfloat16
F32 = jnp.float32
NT = (((1,), (1,)), ((), ()))


def iota(shape, dim):
    return lax.broadcasted_iota(jnp.int32, shape, dim)


def one_hot(condition):
    return jnp.where(condition, 1.0, 0.0).astype(BF16)


def halves(x):
    high = x.astype(BF16)
    return high, (x - high.astype(F32)).astype(BF16)


def dot(a, b):
    return jnp.dot(a, b, preferred_element_type=F32)


def residual_kernel(columns, blocks, before, own, after, loads, info, out, cells, placed, message):
    spread_row, spread_col = iota((B, 768), 0), iota((B, 768), 1)
    spread = one_hot((spread_col == spread_row) | (spread_col == spread_row + 576))

    def place(i, carry):
        parts = []
        for source in (before, own, after, loads):
            parts.extend(halves(source[i]))
        both = dot(jnp.concatenate(parts, axis=0), spread)
        for s in range(4):
            pieces = []
            for part in range(2):
                for v in range(2):
                    row = s * 32 + part * 16 + v * 8
                    pieces.append(both[row:row + 8, :384])
                    pieces.append(both[row:row + 8, 384:])
            cells[s * P_SIZE + i] = jnp.concatenate(pieces, axis=0).astype(BF16)
        return carry

    lax.fori_loop(0, P_SIZE, place, 0)

    unit_row, unit_col = iota((PAIRS, 384), 0), iota((PAIRS, 384), 1)
    pair = (unit_row % 32) * 3 + unit_row // 32
    unit = one_hot((unit_col == 2 * pair) | (unit_col == 2 * pair + B + 1))
    put_row, put_col = iota((32, 512), 0), iota((32, 512), 1)

    placed[...] = jnp.zeros((PAIRS, 512), F32)

    def block_row(g, squares):
        total = lax.dot_general(unit, cells[3 * P_SIZE + g], NT, preferred_element_type=F32)
        low_total = jnp.zeros((PAIRS, 32), F32)
        for j in range(NNZ):
            cell = columns[g, j]
            wide = []
            for k in range(3):
                start = g * 1152 + 12 * k + j
                wide.append(jnp.concatenate(
                    [blocks[pl.ds(start + 4 * t, 32, stride=36), :] for t in range(3)], axis=1))
            high, low = halves(jnp.concatenate(wide, axis=0))
            right = cells[cell]
            total = total - lax.dot_general(high, right, NT, preferred_element_type=F32)
            low_total = low_total + lax.dot_general(low, right[:32], NT, preferred_element_type=F32)
        residual = total[:, :32] + total[:, 32:] - low_total
        put = one_hot(put_col == (put_row // 16) * 256 + (g // 6) * LANES + (g % 6) * 16 + put_row % 16)
        placed[...] += dot(residual.astype(BF16), put)
        return squares + jnp.sum(residual * residual, axis=0, keepdims=True)

    squares = lax.fori_loop(0, P_SIZE, block_row, jnp.zeros((1, 32), F32))
    whole = jnp.sum(squares, axis=1, keepdims=True)
    first = whole.astype(BF16).astype(F32)
    second = (whole - first).astype(BF16).astype(F32)
    third = whole - first - second
    lane = iota((DOM, LANES), 1)
    for v in range(2):
        for k in range(3):
            for t in range(2):
                message[pl.ds(v * 256 + 2 * k + t, 32, stride=ROWS), :] = placed[
                    k * 32:(k + 1) * 32, v * 256 + t * LANES:v * 256 + (t + 1) * LANES]
    message[pl.ds(6, DOM, stride=ROWS), :] = jnp.broadcast_to(info[...], (DOM, LANES))
    message[pl.ds(7, DOM, stride=ROWS), :] = jnp.where(
        lane == 0, first, jnp.where(lane == 1, second, jnp.where(lane == 2, third, 0.0)))
    out[...] = message[...].astype(BF16)


def permute_kernel(received, out, notes, squares, wide, message):
    wide[...] = received[...].astype(F32)
    info = wide[pl.ds(6, DOM, stride=ROWS), :]
    notes[...] = info
    squares[...] = jnp.broadcast_to(jnp.sum(wide[pl.ds(7, DOM, stride=ROWS), :]).reshape(1, 1), (1, LANES))
    rows = jnp.concatenate(
        [wide[pl.ds(s, DOM, stride=ROWS), :].astype(BF16) for s in range(6)], axis=1)
    lane = iota((DOM, LANES), 1)
    source = iota((DOM, DOM), 1).astype(F32)
    place = iota((DOM, 256), 1)
    place = jnp.where(place % LANES < 96, (place // LANES) * 6 + (place % LANES) // 16, -1).astype(F32)
    fold_row, fold_col = iota((256, LANES), 0), iota((256, LANES), 1)
    for t in range(2):
        moved = jnp.zeros((3 * DOM, LANES), F32)
        for i in range(6):
            slot = 6 * t + i
            device = jnp.sum(jnp.where(lane == 64 + slot, info, 0.0), axis=1, keepdims=True)
            row = jnp.sum(jnp.where(lane == 76 + slot, info, 0.0), axis=1, keepdims=True)
            taken = dot(one_hot(device == source), rows)
            keep = row == place
            kept = jnp.concatenate(
                [jnp.where(keep, taken[:, k * 256:(k + 1) * 256], 0.0) for k in range(3)], axis=0)
            fold = one_hot((fold_row % 16 == fold_col % 16) & (fold_col // 16 == i))
            moved = moved + dot(kept.astype(BF16), fold)
        for k in range(3):
            message[pl.ds(2 * k + t, DOM, stride=ROWS), :] = moved[k * DOM:(k + 1) * DOM]
    for s in (6, 7):
        message[pl.ds(s, DOM, stride=ROWS), :] = jnp.zeros((DOM, LANES), F32)
    out[...] = message[...].astype(BF16)


def update_kernel(received, inverses, tiles, level, ancestors, out, wide, leaf, rest, right):
    wide[...] = received[...].astype(F32)
    slabs = []
    for k in range(3):
        slabs.append(jnp.concatenate(
            [wide[pl.ds(v * 256 + 2 * k + t, 32, stride=ROWS), :] for v in range(2) for t in range(2)],
            axis=1))
    slab = jnp.concatenate(slabs, axis=0).astype(BF16)
    row, col = iota((512, 512), 0), iota((512, 512), 1)
    inner = row % LANES
    slot = (row // LANES) % 2 * 6 + inner // 16
    target = (row // 8) % 2 * 256 + slot * 16 + (row // 256) * 8 + row % 8
    spread = dot(slab, one_hot((col == target) & (inner < 96)))
    for k in range(3):
        for par in range(2):
            part = spread[k * 32:(k + 1) * 32, par * 256:(par + 1) * 256]
            leaf[pl.ds(2 * k + par, 32, stride=6), :] = part[:, :LANES]
            rest[pl.ds(2 * k + par, 32, stride=6), :] = part[:, LANES:]

    def doubled(x):
        zeros = jnp.zeros_like(x)
        return jnp.concatenate(
            [jnp.concatenate([x, zeros], axis=1), jnp.concatenate([zeros, x], axis=1)], axis=0)

    def left(ref, start, count):
        return jnp.concatenate(
            [ref[pl.ds(start, count), t].reshape(count * 8, LANES) for t in range(3)], axis=1)

    solved = dot(left(inverses, 0, PAIRS), doubled(leaf[...].astype(BF16)))
    own = iota((768, 256), 0) % 8 == (iota((768, 256), 1) % LANES) // 16
    solved = jnp.where(own, solved, 0.0).astype(BF16)
    gather = one_hot(iota((B, 768), 1) // 8 == iota((B, 768), 0) // 2)
    solved = dot(gather, solved)
    solved = jnp.where(iota((B, LANES), 0) % 2 == 0, solved[:, :LANES], solved[:, LANES:])
    unit = one_hot(iota((LANES, LANES), 0) == iota((LANES, LANES), 1))
    level[...] = lax.dot_general(unit, solved.astype(BF16), NT, preferred_element_type=F32).astype(BF16)
    ancestors[...] = lax.dot_general(
        unit[:64], rest[...].astype(BF16), NT, preferred_element_type=F32)
    owner = iota((B, LANES), 1) // 16
    for k in range(LEAF):
        right[k * 384:(k + 1) * 384] = doubled(jnp.where(owner == k, solved, 0.0)).astype(BF16)
    half = PAIRS // 2
    for h in range(2):
        total = jnp.zeros((half * 8, 256), F32)
        for k in range(LEAF):
            total = total + dot(left(tiles, k * PAIRS + h * half, half), right[k * 384:(k + 1) * 384])
        out[h * half * 8:(h + 1) * half * 8] = total.astype(BF16)


def sum_kernel(received, targets, out):
    select = one_hot(targets[...] == iota((256, 512), 0).astype(F32))
    owner = (iota((64, 256), 1) % LANES) // 16
    group = iota((256, LANES), 1) // 16
    for tile in range(3):
        packed = jnp.zeros((256, LANES), F32)
        for part in range(4):
            pair = tile * 4 + part
            rows = jnp.concatenate(
                [received[s, pair * 8:(pair + 1) * 8, :].astype(F32) for s in range(GROUP)], axis=0)
            right = jnp.concatenate(
                [jnp.where(owner == k, rows, 0.0) for k in range(LEAF)], axis=0).astype(BF16)
            summed = dot(select, right)
            for par in range(2):
                one = summed[:, par * LANES:(par + 1) * LANES]
                for shift in (64, 32, 16):
                    one = one + pltpu.roll(one, shift, 1)
                packed = jnp.where(group == part * 2 + par, one, packed)
        out[:, tile * LANES:(tile + 1) * LANES] = packed.astype(BF16)


def final_kernel(received, ancestors, out):
    place = iota((32, 256), 1)
    source, block = place // ANC, place % ANC
    group = source // (N_Z * N_CORE) * N_CORE + source % N_CORE
    row = iota((32, 256), 0)
    pick = one_hot((row // GROUP == block) & (row % GROUP == group))
    summed = dot(pick, received[...])
    own = iota((CASES, 384), 1) % CASES == iota((CASES, 384), 0)
    to_row, to_col = iota((384, B), 0), iota((384, B), 1)
    total = jnp.zeros((3 * ANC * CASES, B), F32)
    for q in range(GROUP):
        left = jnp.concatenate(
            [jnp.where(own, jnp.broadcast_to(summed[t * GROUP + q:t * GROUP + q + 1], (CASES, 384)), 0.0)
             for t in range(ANC)], axis=0)
        first = left.astype(BF16)
        second, third = halves(left - first.astype(F32))
        total = total + dot(
            jnp.concatenate([first, second, third], axis=0),
            one_hot(to_col == q * 24 + to_row // 16))
    count = ANC * CASES
    out[...] = ancestors[...] - (total[:count] + total[count:2 * count] + total[2 * count:])


def call(kernel, name, shapes, in_specs, scratch, megabytes=16):
    outs = [jax.ShapeDtypeStruct(*s) for s in shapes]
    return pl.pallas_call(
        kernel,
        out_shape=outs,
        in_specs=in_specs,
        out_specs=[pl.BlockSpec(memory_space=pltpu.VMEM)] * len(outs),
        scratch_shapes=scratch,
        compiler_params=pltpu.CompilerParams(vmem_limit_bytes=megabytes * 2**20),
        name=name,
    )


def on_device(solution, loads, blocks, columns, row_source, inverses, tiles, targets):
    vmem = pl.BlockSpec(memory_space=pltpu.VMEM)
    smem = pl.BlockSpec(memory_space=pltpu.SMEM)
    device = lax.axis_index("dom")
    before = lax.ppermute(solution, "dom", [(i, i + 1) for i in range(DOM - 1)])
    after = lax.ppermute(solution, "dom", [(i + 1, i) for i in range(DOM - 1)])
    local = columns - (device * P_SIZE - P_SIZE)
    natural = blocks.reshape(P_SIZE, NNZ, 288, LANES).transpose(0, 2, 1, 3).reshape(P_SIZE * 1152, LANES)
    info = jnp.concatenate([
        targets.reshape(LEAF * UPD), row_source // P_SIZE, row_source % P_SIZE,
        jnp.zeros((LANES - 88,), jnp.int32)]).astype(F32).reshape(1, LANES)
    (message,) = call(
        residual_kernel, "residual", [((DOM * ROWS, LANES), BF16)],
        [smem] + [vmem] * 6,
        [pltpu.VMEM((4 * P_SIZE, 64, 384), BF16), pltpu.VMEM((PAIRS, 512), F32),
         pltpu.VMEM((DOM * ROWS, LANES), F32)], 24,
    )(local, natural, before, solution, after, loads, info)

    def exchange(x):
        x = x.reshape(DOM, ROWS, LANES)
        return lax.all_to_all(x, "dom", 0, 0, tiled=True).reshape(DOM * ROWS, LANES)

    message, notes, squares = call(
        permute_kernel, "permute",
        [((DOM * ROWS, LANES), BF16), ((DOM, LANES), F32), ((1, LANES), F32)], [vmem],
        [pltpu.VMEM((DOM * ROWS, LANES), F32), pltpu.VMEM((DOM * ROWS, LANES), F32)],
    )(exchange(message))
    for step in (1, 2):
        squares = squares + lax.ppermute(squares, "rhs", [(i, i ^ step) for i in range(4)])
    residual_rms = jnp.sqrt(squares[0, 0] / (DOM * P_SIZE * CASES * 4 * B))

    natural_inverses = inverses.reshape(LEAF, 288, LANES).transpose(1, 0, 2).reshape(PAIRS, 3, LEAF, LANES)
    natural_tiles = tiles.reshape(LEAF, UPD, 288, LANES).transpose(0, 2, 1, 3)
    natural_tiles = natural_tiles.reshape(LEAF * PAIRS, 3, UPD, LANES)
    level, ancestors, message = call(
        update_kernel, "update",
        [((LEAF * CASES, B), BF16), ((ANC * CASES, B), F32), ((PAIRS * UPD, 256), BF16)], [vmem] * 3,
        [pltpu.VMEM((DOM * ROWS, LANES), F32), pltpu.VMEM((B, LANES), F32), pltpu.VMEM((B, LANES), F32),
         pltpu.VMEM((LEAF * 384, 256), BF16)], 24,
    )(exchange(message), natural_inverses, natural_tiles)

    groups = [[(x * N_Z + z) * N_CORE + c for x in range(N_X) for c in range(N_CORE)] for z in range(N_Z)]
    received = lax.all_to_all(
        message.reshape(GROUP, 96, 256), "dom", 0, 0, axis_index_groups=groups, tiled=True)
    z = (device // N_CORE) % N_Z
    near = lax.dynamic_index_in_dim(notes.reshape(N_X, N_Z, N_CORE, LANES), z, axis=1, keepdims=False)
    near = near.reshape(GROUP, LANES)[:, :LEAF * UPD].reshape(GROUP, LEAF, UPD)
    near = near.transpose(1, 0, 2).reshape(1, LEAF * GROUP * UPD)
    (sums,) = call(sum_kernel, "sum", [((DOM * ANC, 384), BF16)], [vmem] * 2, [])(received, near)
    sums = lax.all_to_all(sums.reshape(DOM, ANC, 384), "dom", 0, 0, tiled=True)
    (ancestor_rhs,) = call(final_kernel, "final", [((ANC * CASES, B), F32)], [vmem] * 2, [])(
        sums.reshape(DOM * ANC, 384), ancestors)
    return (level.reshape(LEAF, CASES, B), ancestor_rhs.reshape(ANC, CASES, B), residual_rms)


def solution(mesh):
    placed = (
        P("dom", "rhs", None),
        P("dom", "rhs", None),
        P("dom", None, None),
        P("dom", None),
        P("dom"),
        P("dom", None),
        P("dom", None, None),
        P("dom", None),
    )
    return jax.shard_map(
        on_device,
        mesh=mesh,
        in_specs=placed,
        out_specs=(P("dom", "rhs", None), P("dom", "rhs", None), P()),
        check_vma=False,
    )
```

```python
import jax
import jax.numpy as jnp
from jax import lax
from jax.experimental import pallas as pl
from jax.experimental.pallas import tpu as pltpu
from jax.sharding import PartitionSpec as P

B = 192
LEAF = 8
ANC = 4
NNZ = 4
UPD = 8
P_SIZE = 12
CASES = 16
DOM = 64
N_X, N_Z, N_CORE = 4, 8, 2
GROUP = N_X * N_CORE
LANES = 128
ROWS = 8
PAIRS = B // 2
BF16 = jnp.bfloat16
F32 = jnp.float32
NT = (((1,), (1,)), ((), ()))


def iota(shape, dim):
    return lax.broadcasted_iota(jnp.int32, shape, dim)


def one_hot(condition):
    return jnp.where(condition, 1.0, 0.0).astype(BF16)


def halves(x):
    high = x.astype(BF16)
    return high, (x - high.astype(F32)).astype(BF16)


def dot(a, b):
    return jnp.dot(a, b, preferred_element_type=F32)


def put_cells(x, cells, slot):
    wide, narrow = x[:, :LANES], jnp.concatenate([x[:, LANES:], jnp.zeros((CASES, 64), F32)], axis=1)
    lower = iota((CASES, LANES), 1) < 64
    zeros = jnp.zeros((CASES, LANES), F32)
    turned = pltpu.roll(wide, 64, 1)
    lines = (
        (wide, narrow, zeros),
        (zeros, jnp.where(lower, 0.0, turned), jnp.where(lower, turned, pltpu.roll(narrow, 64, 1))),
    )
    for par in range(2):
        for t in range(3):
            for part, value in enumerate(halves(lines[par][t])):
                row = (2 * par + part) * CASES
                cells[slot, row:row + CASES, t * LANES:(t + 1) * LANES] = value


def residual_kernel(table, blocks, before, after, rows, out,
                    wide, cells, load_cells, message, sems):
    count = NNZ * 288
    copies = [pltpu.make_async_copy(blocks.at[pl.ds(g * count, count)], wide.at[pl.ds(g * count, count)],
                                    sems.at[g]) for g in range(P_SIZE)]
    for copy in copies:
        copy.start()

    for i in range(P_SIZE):
        put_cells(before[i], cells, i)
        put_cells(rows[i], cells, P_SIZE + i)
        put_cells(after[i], cells, 2 * P_SIZE + i)
        put_cells(rows[P_SIZE + i], load_cells, i)

    unit_row, unit_col = iota((PAIRS, 384), 0), iota((PAIRS, 384), 1)
    pair = (unit_row % 32) * 3 + unit_row // 32
    unit = one_hot((unit_col == 2 * pair) | (unit_col == 2 * pair + B + 1))
    residuals = ([], [])
    for g in range(P_SIZE):
        if g % 3 == 0:
            for copy in copies[g:g + 3]:
                copy.wait()
        high, low = [], []
        for j in range(NNZ):
            for t in range(3):
                tall = jnp.concatenate(
                    [wide[pl.ds(g * count + 12 * k + j + 4 * t, 32, stride=36), :] for k in range(3)], axis=0)
                first, second = halves(tall)
                high.append(first)
                low.append(second)
        right = jnp.concatenate([cells[table[j, g]] for j in range(NNZ)], axis=1)
        total = lax.dot_general(unit, load_cells[g], NT, preferred_element_type=F32)
        for side in (high, low):
            total = total - lax.dot_general(
                jnp.concatenate(side, axis=1), right, NT, preferred_element_type=F32)
        for par in range(2):
            one = total[:, par * 32:par * 32 + 16] + total[:, par * 32 + 16:par * 32 + 32]
            residuals[par].append(one)

    lane = iota((ROWS, LANES), 1)
    info = jnp.zeros((ROWS, LANES), jnp.int32)
    for k in range(LEAF):
        for m in range(UPD):
            info = jnp.where(lane == k * UPD + m, table[8 + k, m], info)
    for i in range(P_SIZE):
        source = table[4, i]
        info = jnp.where(lane == 64 + i, source // P_SIZE, info)
        info = jnp.where(lane == 76 + i, source % P_SIZE, info)
    info = info.astype(F32)[:1]
    squares = jnp.zeros((PAIRS, LANES), F32)
    for par in range(2):
        ones = residuals[par] + [jnp.zeros((PAIRS, CASES), F32)] * 4
        for t in range(2):
            tile = jnp.concatenate(ones[8 * t:8 * t + 8], axis=1)
            squares = squares + tile * tile
            for k in range(3):
                message[pl.ds(par * 256 + 2 * k + t, 32, stride=ROWS), :] = tile[k * 32:(k + 1) * 32]
    whole = jnp.sum(squares).reshape(1, 1)
    first = whole.astype(BF16).astype(F32)
    second = (whole - first).astype(BF16).astype(F32)
    third = whole - first - second
    lane = iota((DOM, LANES), 1)
    message[pl.ds(6, DOM, stride=ROWS), :] = jnp.broadcast_to(info, (DOM, LANES))
    message[pl.ds(7, DOM, stride=ROWS), :] = jnp.where(
        lane == 0, first, jnp.where(lane == 1, second, jnp.where(lane == 2, third, 0.0)))
    out[...] = message[...].astype(BF16)


def permute_kernel(received, out, notes, squares, wide, message):
    wide[...] = received[...].astype(F32)
    info = wide[pl.ds(6, DOM, stride=ROWS), :]
    notes[...] = info
    squares[...] = jnp.broadcast_to(jnp.sum(wide[pl.ds(7, DOM, stride=ROWS), :]).reshape(1, 1), (1, LANES))
    rows = jnp.concatenate(
        [wide[pl.ds(s, DOM, stride=ROWS), :].astype(BF16) for s in range(6)], axis=1)
    lane = iota((DOM, LANES), 1)
    source = iota((DOM, DOM), 1).astype(F32)
    place = (iota((DOM, 256), 1) // CASES).astype(F32)
    chosen, keep = [], []
    for i in range(P_SIZE):
        device = jnp.sum(jnp.where(lane == 64 + i, info, 0.0), axis=1, keepdims=True)
        row = jnp.sum(jnp.where(lane == 76 + i, info, 0.0), axis=1, keepdims=True)
        chosen.append(one_hot(device == source))
        keep.append(row == place)
    taken = dot(jnp.concatenate(chosen, axis=0), rows)
    fold = one_hot(iota((256, LANES), 0) % CASES == iota((256, LANES), 1) % CASES)
    for k in range(3):
        kept = jnp.concatenate(
            [jnp.where(keep[i], taken[i * DOM:(i + 1) * DOM, k * 256:(k + 1) * 256], 0.0).astype(BF16)
             for i in range(P_SIZE)], axis=0)
        copies = dot(kept, fold)
        for t, count in ((0, LEAF), (1, ANC)):
            moved = jnp.zeros((DOM, LANES), F32)
            for i in range(count):
                at = (LEAF * t + i) * DOM
                moved = jnp.where(lane // CASES == i, copies[at:at + DOM], moved)
            message[pl.ds(2 * k + t, DOM, stride=ROWS), :] = moved
    for s in (6, 7):
        message[pl.ds(s, DOM, stride=ROWS), :] = jnp.zeros((DOM, LANES), F32)
    out[...] = message[...].astype(BF16)


def update_kernel(received, inverses, tiles, squares, level, ancestors, out, squares_out,
                  wide, leaf, rest, right, near, sems, partial):
    copies = [pltpu.make_async_copy(tiles.at[pl.ds(k * PAIRS, PAIRS)], near.at[pl.ds(k * PAIRS, PAIRS)],
                                    sems.at[k]) for k in range(LEAF)]
    for copy in copies:
        copy.start()
    squares_out[...] = squares[...]
    wide[...] = received[...].astype(F32)
    for k in range(3):
        for par in range(2):
            at = pl.ds(2 * k + par, 32, stride=6)
            leaf[at, :] = wide[pl.ds(par * 256 + 2 * k, 32, stride=ROWS), :]
            rest[at, :] = wide[pl.ds(par * 256 + 2 * k + 1, 32, stride=ROWS), :]

    def doubled(x):
        zeros = jnp.zeros_like(x)
        return jnp.concatenate(
            [jnp.concatenate([x, zeros], axis=1), jnp.concatenate([zeros, x], axis=1)], axis=0)

    def left(ref, start, count):
        return jnp.concatenate(
            [ref[pl.ds(start, count), t].reshape(count * 8, LANES) for t in range(3)], axis=1)

    solved = dot(left(inverses, 0, PAIRS), doubled(leaf[...].astype(BF16)))
    own = iota((768, 256), 0) % 8 == (iota((768, 256), 1) % LANES) // 16
    solved = jnp.where(own, solved, 0.0).astype(BF16)
    gather = one_hot(iota((B, 768), 1) // 8 == iota((B, 768), 0) // 2)
    solved = dot(gather, solved)
    solved = jnp.where(iota((B, LANES), 0) % 2 == 0, solved[:, :LANES], solved[:, LANES:])
    unit = one_hot(iota((LANES, LANES), 0) == iota((LANES, LANES), 1))
    level[...] = lax.dot_general(unit, solved.astype(BF16), NT, preferred_element_type=F32).astype(BF16)
    ancestors[...] = lax.dot_general(
        unit[:64], rest[...].astype(BF16), NT, preferred_element_type=F32)
    owner = iota((B, LANES), 1) // 16
    for k in range(LEAF):
        right[k * 384:(k + 1) * 384] = doubled(jnp.where(owner == k, solved, 0.0)).astype(BF16)
    step, band = LEAF // 2, PAIRS // 2
    for first in range(0, LEAF, step):
        for copy in copies[first:first + step]:
            copy.wait()
        for r in range(0, PAIRS, band):
            at = slice(r * 8, (r + band) * 8)
            wide_left = jnp.concatenate(
                [left(near, k * PAIRS + r, band) for k in range(first, first + step)], axis=1)
            total = dot(wide_left, right[first * 384:(first + step) * 384])
            if first == 0:
                partial[at] = total
            else:
                out[at] = (partial[at] + total).astype(BF16)


def sum_kernel(received, targets, squares, out, squares_out, right):
    squares_out[...] = squares[...]
    select = one_hot(targets[...] == iota((256, 512), 0).astype(F32))
    group = iota((64, LANES), 1) // CASES
    for tile in range(3):
        parts = []
        for pair in range(tile * 4, tile * 4 + 4):
            rows = jnp.concatenate(
                [received[s, pair * 8:(pair + 1) * 8, :].astype(F32) for s in range(GROUP)], axis=0)
            parts.extend([rows[:, :LANES], rows[:, LANES:]])
        for step in (4, 2, 1):
            upper = (group // step) % 2 == 1
            turned = list(parts)
            for i in range(8):
                if not i & step:
                    a, b = parts[i], parts[i + step]
                    turned[i] = jnp.where(upper, pltpu.roll(b, step * CASES, 1), a)
                    turned[i + step] = jnp.where(upper, b, pltpu.roll(a, LANES - step * CASES, 1))
            parts = turned
        for k in range(LEAF):
            right[k * 64:(k + 1) * 64, tile * LANES:(tile + 1) * LANES] = parts[k].astype(BF16)
    out[...] = dot(select, right[...]).reshape(DOM, ANC, 384).astype(BF16)


def final_kernel(received, ancestors, out):
    place = iota((32, 256), 1)
    source, block = place // ANC, place % ANC
    group = source // (N_Z * N_CORE) * N_CORE + source % N_CORE
    row = iota((32, 256), 0)
    pick = one_hot((row // GROUP == block) & (row % GROUP == group))
    summed = dot(pick, received[...])
    own = iota((CASES, 384), 1) % CASES == iota((CASES, 384), 0)
    to_row, to_col = iota((384, B), 0), iota((384, B), 1)
    total = jnp.zeros((3 * ANC * CASES, B), F32)
    for q in range(GROUP):
        left = jnp.concatenate(
            [jnp.where(own, jnp.broadcast_to(summed[t * GROUP + q:t * GROUP + q + 1], (CASES, 384)), 0.0)
             for t in range(ANC)], axis=0)
        first = left.astype(BF16)
        second, third = halves(left - first.astype(F32))
        total = total + dot(
            jnp.concatenate([first, second, third], axis=0),
            one_hot(to_col == q * 24 + to_row // 16))
    count = ANC * CASES
    out[...] = ancestors[...] - (total[:count] + total[count:2 * count] + total[2 * count:])


def call(kernel, name, shapes, in_specs, scratch, megabytes=16, cost=None):
    outs = [jax.ShapeDtypeStruct(*s) for s in shapes]
    return pl.pallas_call(
        kernel,
        out_shape=outs,
        in_specs=in_specs,
        out_specs=[pl.BlockSpec(memory_space=pltpu.VMEM)] * len(outs),
        scratch_shapes=scratch,
        compiler_params=pltpu.CompilerParams(vmem_limit_bytes=megabytes * 2**20),
        cost_estimate=cost,
        name=name,
    )


def on_device(solution, loads, blocks, columns, row_source, inverses, tiles, targets):
    vmem = pl.BlockSpec(memory_space=pltpu.VMEM)
    smem = pl.BlockSpec(memory_space=pltpu.SMEM)
    hbm = pl.BlockSpec(memory_space=pltpu.HBM)
    dma = pltpu.SemaphoreType.DMA
    device = lax.axis_index("dom")
    before = lax.ppermute(solution, "dom", [(i, i + 1) for i in range(DOM - 1)])
    after = lax.ppermute(solution, "dom", [(i + 1, i) for i in range(DOM - 1)])
    table = jnp.concatenate([
        jnp.pad(columns.T - (device * P_SIZE - P_SIZE), ((0, 0), (0, LANES - P_SIZE))),
        jnp.pad(row_source.reshape(1, P_SIZE), ((0, 3), (0, LANES - P_SIZE))),
        jnp.pad(targets, ((0, 0), (0, LANES - UPD)))], axis=0)
    natural = blocks.reshape(P_SIZE, NNZ, 288, LANES).transpose(0, 2, 1, 3).reshape(P_SIZE * 1152, LANES)
    natural_inverses = inverses.reshape(LEAF, 288, LANES).transpose(1, 0, 2).reshape(PAIRS, 3, LEAF, LANES)
    natural_tiles = tiles.reshape(LEAF, UPD, 288, LANES).transpose(0, 2, 1, 3)
    natural_tiles = natural_tiles.reshape(LEAF * PAIRS, 3, UPD, LANES)
    (message,) = call(
        residual_kernel, "residual", [((DOM * ROWS, LANES), BF16)],
        [smem, hbm] + [vmem] * 3,
        [pltpu.VMEM((P_SIZE * 1152, LANES), F32),
         pltpu.VMEM((3 * P_SIZE, 64, 384), BF16), pltpu.VMEM((P_SIZE, 64, 384), BF16),
         pltpu.VMEM((DOM * ROWS, LANES), F32), dma((P_SIZE,))], 50,
    )(table, natural, before, after,
      jnp.concatenate([solution, loads], axis=0))

    def exchange(x):
        x = x.reshape(DOM, ROWS, LANES)
        return lax.all_to_all(x, "dom", 0, 0, tiled=True).reshape(DOM * ROWS, LANES)

    def across(x, step):
        return x + lax.ppermute(x, "rhs", [(i, i ^ step) for i in range(4)])

    message, notes, squares = call(
        permute_kernel, "permute",
        [((DOM * ROWS, LANES), BF16), ((DOM, LANES), F32), ((1, LANES), F32)], [vmem],
        [pltpu.VMEM((DOM * ROWS, LANES), F32), pltpu.VMEM((DOM * ROWS, LANES), F32)], 16,
        pl.CostEstimate(flops=4 * 10**9, bytes_accessed=10**6, transcendentals=0),
    )(exchange(message))

    level, ancestors, message, squares = call(
        update_kernel, "update",
        [((LEAF * CASES, B), BF16), ((ANC * CASES, B), F32), ((PAIRS * UPD, 256), BF16), ((1, LANES), F32)],
        [vmem, vmem, hbm, vmem],
        [pltpu.VMEM((DOM * ROWS, LANES), F32), pltpu.VMEM((B, LANES), F32), pltpu.VMEM((B, LANES), F32),
         pltpu.VMEM((LEAF * 384, 256), BF16), pltpu.VMEM((LEAF * PAIRS, 3, UPD, LANES), BF16),
         dma((LEAF,)), pltpu.VMEM((PAIRS * UPD, 256), F32)], 52,
    )(exchange(message), natural_inverses, natural_tiles, across(squares, 1))

    groups = [[(x * N_Z + z) * N_CORE + c for x in range(N_X) for c in range(N_CORE)] for z in range(N_Z)]
    received = lax.all_to_all(
        message.reshape(GROUP, 96, 256), "dom", 0, 0, axis_index_groups=groups, tiled=True)
    z = (device // N_CORE) % N_Z
    near = lax.dynamic_index_in_dim(notes.reshape(N_X, N_Z, N_CORE, LANES), z, axis=1, keepdims=False)
    near = near.reshape(GROUP, LANES)[:, :LEAF * UPD].reshape(GROUP, LEAF, UPD)
    near = near.transpose(1, 0, 2).reshape(1, LEAF * GROUP * UPD)
    sums, squares = call(
        sum_kernel, "sum", [((DOM, ANC, 384), BF16), ((1, LANES), F32)], [vmem] * 3,
        [pltpu.VMEM((512, 384), BF16)],
    )(received, near, across(squares, 2))
    residual_rms = jnp.sqrt(squares[0, 0] / (DOM * P_SIZE * CASES * 4 * B))
    sums = lax.all_to_all(sums, "dom", 0, 0, tiled=True)
    (ancestor_rhs,) = call(final_kernel, "final", [((ANC * CASES, B), F32)], [vmem] * 2, [])(
        sums.reshape(DOM * ANC, 384), ancestors)
    return (level.reshape(LEAF, CASES, B), ancestor_rhs.reshape(ANC, CASES, B), residual_rms)


def solution(mesh):
    placed = (
        P("dom", "rhs", None),
        P("dom", "rhs", None),
        P("dom", None, None),
        P("dom", None),
        P("dom"),
        P("dom", None),
        P("dom", None, None),
        P("dom", None),
    )
    return jax.shard_map(
        on_device,
        mesh=mesh,
        in_specs=placed,
        out_specs=(P("dom", "rhs", None), P("dom", "rhs", None), P()),
        check_vma=False,
    )
```

```python
import jax
import jax.numpy as jnp
from jax import lax
from jax.experimental import pallas as pl
from jax.experimental.pallas import tpu as pltpu
from jax.sharding import PartitionSpec as P

B = 192
LEAF = 8
ANC = 4
NNZ = 4
UPD = 8
P_SIZE = 12
CASES = 16
DOM = 64
N_X, N_Z, N_CORE = 4, 8, 2
GROUP = N_X * N_CORE
LANES = 128
ROWS = 8
PAIRS = B // 2
BF16 = jnp.bfloat16
F32 = jnp.float32
NT = (((1,), (1,)), ((), ()))


def iota(shape, dim):
    return lax.broadcasted_iota(jnp.int32, shape, dim)


def one_hot(condition):
    return jnp.where(condition, 1.0, 0.0).astype(BF16)


def halves(x):
    high = x.astype(BF16)
    return high, (x - high.astype(F32)).astype(BF16)


def dot(a, b):
    return jnp.dot(a, b, preferred_element_type=F32)


def put_cells(x, cells, slot):
    wide, narrow = x[:, :LANES], jnp.concatenate([x[:, LANES:], jnp.zeros((CASES, 64), F32)], axis=1)
    lower = iota((CASES, LANES), 1) < 64
    zeros = jnp.zeros((CASES, LANES), F32)
    turned = pltpu.roll(wide, 64, 1)
    lines = (
        (wide, narrow, zeros),
        (zeros, jnp.where(lower, 0.0, turned), jnp.where(lower, turned, pltpu.roll(narrow, 64, 1))),
    )
    for par in range(2):
        for t in range(3):
            for part, value in enumerate(halves(lines[par][t])):
                row = (2 * par + part) * CASES
                cells[slot, row:row + CASES, t * LANES:(t + 1) * LANES] = value


def lane_kernel(out):
    out[...] = iota((ROWS, LANES), 1)


def residual_kernel(table, blocks, chip, far, own, loads, lanes, out,
                    wide, cells, load_cells, message, sems):
    count = NNZ * 288
    copies = [pltpu.make_async_copy(blocks.at[pl.ds(g * count, count)], wide.at[pl.ds(g * count, count)],
                                    sems.at[g]) for g in range(P_SIZE)]
    for copy in copies:
        copy.start()

    for i in range(P_SIZE):
        put_cells(chip[i], cells, i)
        put_cells(own[i], cells, P_SIZE + i)
        put_cells(far[i], cells, 2 * P_SIZE + i)
        put_cells(loads[i], load_cells, i)

    unit_row, unit_col = iota((PAIRS, 384), 0), iota((PAIRS, 384), 1)
    pair = (unit_row % 32) * 3 + unit_row // 32
    unit = one_hot((unit_col == 2 * pair) | (unit_col == 2 * pair + B + 1))
    residuals = ([], [])
    for g in range(P_SIZE):
        if g % 3 == 0:
            for copy in copies[g:g + 3]:
                copy.wait()
        high, low = [], []
        for j in range(NNZ):
            for t in range(3):
                tall = jnp.concatenate(
                    [wide[pl.ds(g * count + 12 * k + j + 4 * t, 32, stride=36), :] for k in range(3)], axis=0)
                first, second = halves(tall)
                high.append(first)
                low.append(second)
        right = jnp.concatenate([cells[table[j, g]] for j in range(NNZ)], axis=1)
        total = lax.dot_general(unit, load_cells[g], NT, preferred_element_type=F32)
        for side in (high, low):
            total = total - lax.dot_general(
                jnp.concatenate(side, axis=1), right, NT, preferred_element_type=F32)
        for par in range(2):
            one = total[:, par * 32:par * 32 + 16] + total[:, par * 32 + 16:par * 32 + 32]
            residuals[par].append(one)

    lane = lanes[...]
    info = jnp.zeros((ROWS, LANES), jnp.int32)
    for k in range(LEAF):
        for m in range(UPD):
            info = jnp.where(lane == k * UPD + m, table[8 + k, m], info)
    for i in range(P_SIZE):
        source = table[4, i]
        info = jnp.where(lane == 64 + i, source // P_SIZE, info)
        info = jnp.where(lane == 76 + i, source % P_SIZE, info)
    info = info.astype(F32)[:1]
    squares = jnp.zeros((PAIRS, LANES), F32)
    for par in range(2):
        ones = residuals[par] + [jnp.zeros((PAIRS, CASES), F32)] * 4
        for t in range(2):
            tile = jnp.concatenate(ones[8 * t:8 * t + 8], axis=1)
            squares = squares + tile * tile
            for k in range(3):
                message[pl.ds(par * 256 + 2 * k + t, 32, stride=ROWS), :] = tile[k * 32:(k + 1) * 32]
    whole = jnp.sum(squares).reshape(1, 1)
    first = whole.astype(BF16).astype(F32)
    second = (whole - first).astype(BF16).astype(F32)
    third = whole - first - second
    lane = iota((DOM, LANES), 1)
    message[pl.ds(6, DOM, stride=ROWS), :] = jnp.broadcast_to(info, (DOM, LANES))
    message[pl.ds(7, DOM, stride=ROWS), :] = jnp.where(
        lane == 0, first, jnp.where(lane == 1, second, jnp.where(lane == 2, third, 0.0)))
    out[...] = message[...].astype(BF16)


def permute_kernel(received, out, notes, squares, wide, message):
    wide[...] = received[...].astype(F32)
    info = wide[pl.ds(6, DOM, stride=ROWS), :]
    notes[...] = info
    squares[...] = jnp.broadcast_to(jnp.sum(wide[pl.ds(7, DOM, stride=ROWS), :]).reshape(1, 1), (1, LANES))
    rows = jnp.concatenate(
        [wide[pl.ds(s, DOM, stride=ROWS), :].astype(BF16) for s in range(6)], axis=1)
    lane = iota((DOM, LANES), 1)
    source = iota((DOM, DOM), 1).astype(F32)
    place = (iota((DOM, 256), 1) // CASES).astype(F32)
    chosen, keep = [], []
    for i in range(P_SIZE):
        device = jnp.sum(jnp.where(lane == 64 + i, info, 0.0), axis=1, keepdims=True)
        row = jnp.sum(jnp.where(lane == 76 + i, info, 0.0), axis=1, keepdims=True)
        chosen.append(one_hot(device == source))
        keep.append(row == place)
    taken = dot(jnp.concatenate(chosen, axis=0), rows)
    fold = one_hot(iota((256, LANES), 0) % CASES == iota((256, LANES), 1) % CASES)
    for k in range(3):
        kept = jnp.concatenate(
            [jnp.where(keep[i], taken[i * DOM:(i + 1) * DOM, k * 256:(k + 1) * 256], 0.0).astype(BF16)
             for i in range(P_SIZE)], axis=0)
        copies = dot(kept, fold)
        for t, count in ((0, LEAF), (1, ANC)):
            moved = jnp.zeros((DOM, LANES), F32)
            for i in range(count):
                at = (LEAF * t + i) * DOM
                moved = jnp.where(lane // CASES == i, copies[at:at + DOM], moved)
            message[pl.ds(2 * k + t, DOM, stride=ROWS), :] = moved
    for s in (6, 7):
        message[pl.ds(s, DOM, stride=ROWS), :] = jnp.zeros((DOM, LANES), F32)
    out[...] = message[...].astype(BF16)


def update_kernel(received, inverses, tiles, squares, level, ancestors, out, squares_out,
                  wide, leaf, rest, right, near, sems, partial):
    copies = [pltpu.make_async_copy(tiles.at[pl.ds(k * PAIRS, PAIRS)], near.at[pl.ds(k * PAIRS, PAIRS)],
                                    sems.at[k]) for k in range(LEAF)]
    for copy in copies:
        copy.start()
    squares_out[...] = squares[...]
    wide[...] = received[...].astype(F32)
    for k in range(3):
        for par in range(2):
            at = pl.ds(2 * k + par, 32, stride=6)
            leaf[at, :] = wide[pl.ds(par * 256 + 2 * k, 32, stride=ROWS), :]
            rest[at, :] = wide[pl.ds(par * 256 + 2 * k + 1, 32, stride=ROWS), :]

    def doubled(x):
        zeros = jnp.zeros_like(x)
        return jnp.concatenate(
            [jnp.concatenate([x, zeros], axis=1), jnp.concatenate([zeros, x], axis=1)], axis=0)

    def left(ref, start, count):
        return jnp.concatenate(
            [ref[pl.ds(start, count), t].reshape(count * 8, LANES) for t in range(3)], axis=1)

    solved = dot(left(inverses, 0, PAIRS), doubled(leaf[...].astype(BF16)))
    own = iota((768, 256), 0) % 8 == (iota((768, 256), 1) % LANES) // 16
    solved = jnp.where(own, solved, 0.0).astype(BF16)
    gather = one_hot(iota((B, 768), 1) // 8 == iota((B, 768), 0) // 2)
    solved = dot(gather, solved)
    solved = jnp.where(iota((B, LANES), 0) % 2 == 0, solved[:, :LANES], solved[:, LANES:])
    unit = one_hot(iota((LANES, LANES), 0) == iota((LANES, LANES), 1))
    level[...] = lax.dot_general(unit, solved.astype(BF16), NT, preferred_element_type=F32).astype(BF16)
    ancestors[...] = lax.dot_general(
        unit[:64], rest[...].astype(BF16), NT, preferred_element_type=F32)
    owner = iota((B, LANES), 1) // 16
    for k in range(LEAF):
        right[k * 384:(k + 1) * 384] = doubled(jnp.where(owner == k, solved, 0.0)).astype(BF16)
    step, band = LEAF // 2, PAIRS // 2
    for first in range(0, LEAF, step):
        for copy in copies[first:first + step]:
            copy.wait()
        for r in range(0, PAIRS, band):
            at = slice(r * 8, (r + band) * 8)
            wide_left = jnp.concatenate(
                [left(near, k * PAIRS + r, band) for k in range(first, first + step)], axis=1)
            total = dot(wide_left, right[first * 384:(first + step) * 384])
            if first == 0:
                partial[at] = total
            else:
                out[at] = (partial[at] + total).astype(BF16)


def sum_kernel(received, targets, squares, out, squares_out, right):
    squares_out[...] = squares[...]
    select = one_hot(targets[...] == iota((256, 512), 0).astype(F32))
    group = iota((64, LANES), 1) // CASES
    for tile in range(3):
        parts = []
        for pair in range(tile * 4, tile * 4 + 4):
            rows = jnp.concatenate(
                [received[s, pair * 8:(pair + 1) * 8, :].astype(F32) for s in range(GROUP)], axis=0)
            parts.extend([rows[:, :LANES], rows[:, LANES:]])
        for step in (4, 2, 1):
            upper = (group // step) % 2 == 1
            turned = list(parts)
            for i in range(8):
                if not i & step:
                    a, b = parts[i], parts[i + step]
                    turned[i] = jnp.where(upper, pltpu.roll(b, step * CASES, 1), a)
                    turned[i + step] = jnp.where(upper, b, pltpu.roll(a, LANES - step * CASES, 1))
            parts = turned
        for k in range(LEAF):
            right[k * 64:(k + 1) * 64, tile * LANES:(tile + 1) * LANES] = parts[k].astype(BF16)
    out[...] = dot(select, right[...]).reshape(DOM, ANC, 384).astype(BF16)


def final_kernel(received, ancestors, out):
    place = iota((32, 256), 1)
    source, block = place // ANC, place % ANC
    group = source // (N_Z * N_CORE) * N_CORE + source % N_CORE
    row = iota((32, 256), 0)
    pick = one_hot((row // GROUP == block) & (row % GROUP == group))
    summed = dot(pick, received[...])
    own = iota((CASES, 384), 1) % CASES == iota((CASES, 384), 0)
    to_row, to_col = iota((384, B), 0), iota((384, B), 1)
    total = jnp.zeros((3 * ANC * CASES, B), F32)
    for q in range(GROUP):
        left = jnp.concatenate(
            [jnp.where(own, jnp.broadcast_to(summed[t * GROUP + q:t * GROUP + q + 1], (CASES, 384)), 0.0)
             for t in range(ANC)], axis=0)
        first = left.astype(BF16)
        second, third = halves(left - first.astype(F32))
        total = total + dot(
            jnp.concatenate([first, second, third], axis=0),
            one_hot(to_col == q * 24 + to_row // 16))
    count = ANC * CASES
    out[...] = ancestors[...] - (total[:count] + total[count:2 * count] + total[2 * count:])


def call(kernel, name, shapes, in_specs, scratch, megabytes=16, cost=None):
    outs = [jax.ShapeDtypeStruct(*s) for s in shapes]
    return pl.pallas_call(
        kernel,
        out_shape=outs,
        in_specs=in_specs,
        out_specs=[pl.BlockSpec(memory_space=pltpu.VMEM)] * len(outs),
        scratch_shapes=scratch,
        compiler_params=pltpu.CompilerParams(vmem_limit_bytes=megabytes * 2**20),
        cost_estimate=cost,
        name=name,
    )


def on_device(solution, loads, blocks, columns, row_source, inverses, tiles, targets):
    vmem = pl.BlockSpec(memory_space=pltpu.VMEM)
    smem = pl.BlockSpec(memory_space=pltpu.SMEM)
    hbm = pl.BlockSpec(memory_space=pltpu.HBM)
    dma = pltpu.SemaphoreType.DMA
    device = lax.axis_index("dom")
    far = lax.ppermute(solution, "dom", [(i, i + 1 if i % 2 else i - 1) for i in range(1, DOM - 1)])
    chip = lax.ppermute(solution, "dom", [(i, i ^ 1) for i in range(DOM)])
    local = columns.T - (device * P_SIZE - P_SIZE)
    turn = jnp.where(local < P_SIZE, 2 * P_SIZE, jnp.where(local < 2 * P_SIZE, 0, -2 * P_SIZE))
    local = local + jnp.where(device % 2 == 0, turn, 0)
    table = jnp.concatenate([
        jnp.pad(local, ((0, 0), (0, LANES - P_SIZE))),
        jnp.pad(row_source.reshape(1, P_SIZE), ((0, 3), (0, LANES - P_SIZE))),
        jnp.pad(targets, ((0, 0), (0, LANES - UPD)))], axis=0)
    natural = blocks.reshape(P_SIZE, NNZ, 288, LANES).transpose(0, 2, 1, 3).reshape(P_SIZE * 1152, LANES)
    natural_inverses = inverses.reshape(LEAF, 288, LANES).transpose(1, 0, 2).reshape(PAIRS, 3, LEAF, LANES)
    natural_tiles = tiles.reshape(LEAF, UPD, 288, LANES).transpose(0, 2, 1, 3)
    natural_tiles = natural_tiles.reshape(LEAF * PAIRS, 3, UPD, LANES)
    (lanes,) = call(
        lane_kernel, "lanes", [((ROWS, LANES), jnp.int32)], [], [], 16,
        pl.CostEstimate(flops=3 * 10**10, bytes_accessed=10**6, transcendentals=0))()
    (message,) = call(
        residual_kernel, "residual", [((DOM * ROWS, LANES), BF16)],
        [smem, hbm] + [vmem] * 5,
        [pltpu.VMEM((P_SIZE * 1152, LANES), F32),
         pltpu.VMEM((3 * P_SIZE, 64, 384), BF16), pltpu.VMEM((P_SIZE, 64, 384), BF16),
         pltpu.VMEM((DOM * ROWS, LANES), F32), dma((P_SIZE,))], 50,
    )(table, natural, chip, far, solution, loads, lanes)

    def exchange(x):
        x = x.reshape(DOM, ROWS, LANES)
        return lax.all_to_all(x, "dom", 0, 0, tiled=True).reshape(DOM * ROWS, LANES)

    def across(x, step):
        return x + lax.ppermute(x, "rhs", [(i, i ^ step) for i in range(4)])

    message, notes, squares = call(
        permute_kernel, "permute",
        [((DOM * ROWS, LANES), BF16), ((DOM, LANES), F32), ((1, LANES), F32)], [vmem],
        [pltpu.VMEM((DOM * ROWS, LANES), F32), pltpu.VMEM((DOM * ROWS, LANES), F32)], 16,
        pl.CostEstimate(flops=4 * 10**9, bytes_accessed=10**6, transcendentals=0),
    )(exchange(message))

    level, ancestors, message, squares = call(
        update_kernel, "update",
        [((LEAF * CASES, B), BF16), ((ANC * CASES, B), F32), ((PAIRS * UPD, 256), BF16), ((1, LANES), F32)],
        [vmem, vmem, hbm, vmem],
        [pltpu.VMEM((DOM * ROWS, LANES), F32), pltpu.VMEM((B, LANES), F32), pltpu.VMEM((B, LANES), F32),
         pltpu.VMEM((LEAF * 384, 256), BF16), pltpu.VMEM((LEAF * PAIRS, 3, UPD, LANES), BF16),
         dma((LEAF,)), pltpu.VMEM((PAIRS * UPD, 256), F32)], 52,
    )(exchange(message), natural_inverses, natural_tiles, across(squares, 1))

    groups = [[(x * N_Z + z) * N_CORE + c for x in range(N_X) for c in range(N_CORE)] for z in range(N_Z)]
    received = lax.all_to_all(
        message.reshape(GROUP, 96, 256), "dom", 0, 0, axis_index_groups=groups, tiled=True)
    z = (device // N_CORE) % N_Z
    near = lax.dynamic_index_in_dim(notes.reshape(N_X, N_Z, N_CORE, LANES), z, axis=1, keepdims=False)
    near = near.reshape(GROUP, LANES)[:, :LEAF * UPD].reshape(GROUP, LEAF, UPD)
    near = near.transpose(1, 0, 2).reshape(1, LEAF * GROUP * UPD)
    sums, squares = call(
        sum_kernel, "sum", [((DOM, ANC, 384), BF16), ((1, LANES), F32)], [vmem] * 3,
        [pltpu.VMEM((512, 384), BF16)],
    )(received, near, across(squares, 2))
    residual_rms = jnp.sqrt(squares[0, 0] / (DOM * P_SIZE * CASES * 4 * B))
    sums = lax.all_to_all(sums, "dom", 0, 0, tiled=True)
    (ancestor_rhs,) = call(final_kernel, "final", [((ANC * CASES, B), F32)], [vmem] * 2, [])(
        sums.reshape(DOM * ANC, 384), ancestors)
    return (level.reshape(LEAF, CASES, B), ancestor_rhs.reshape(ANC, CASES, B), residual_rms)


def solution(mesh):
    placed = (
        P("dom", "rhs", None),
        P("dom", "rhs", None),
        P("dom", None, None),
        P("dom", None),
        P("dom"),
        P("dom", None),
        P("dom", None, None),
        P("dom", None),
    )
    return jax.shard_map(
        on_device,
        mesh=mesh,
        in_specs=placed,
        out_specs=(P("dom", "rhs", None), P("dom", "rhs", None), P()),
        check_vma=False,
    )
```

```python
import jax
import jax.numpy as jnp
from jax import lax
from jax.experimental import pallas as pl
from jax.experimental.pallas import tpu as pltpu
from jax.sharding import PartitionSpec as P

B = 192
LEAF = 8
ANC = 4
NNZ = 4
UPD = 8
P_SIZE = 12
CASES = 16
DOM = 64
N_X, N_Z, N_CORE = 4, 8, 2
GROUP = N_X * N_CORE
LANES = 128
ROWS = 8
PAIRS = B // 2
BF16 = jnp.bfloat16
F32 = jnp.float32
NT = (((1,), (1,)), ((), ()))


def iota(shape, dim):
    return lax.broadcasted_iota(jnp.int32, shape, dim)


def one_hot(condition):
    return jnp.where(condition, 1.0, 0.0).astype(BF16)


def halves(x):
    high = x.astype(BF16)
    return high, (x - high.astype(F32)).astype(BF16)


def dot(a, b):
    return jnp.dot(a, b, preferred_element_type=F32)


def put_cells(x, cells, slot):
    wide, narrow = x[:, :LANES], jnp.concatenate([x[:, LANES:], jnp.zeros((CASES, 64), F32)], axis=1)
    lower = iota((CASES, LANES), 1) < 64
    zeros = jnp.zeros((CASES, LANES), F32)
    turned = pltpu.roll(wide, 64, 1)
    lines = (
        (wide, narrow, zeros),
        (zeros, jnp.where(lower, 0.0, turned), jnp.where(lower, turned, pltpu.roll(narrow, 64, 1))),
    )
    for par in range(2):
        for t in range(3):
            for part, value in enumerate(halves(lines[par][t])):
                row = (2 * par + part) * CASES
                cells[slot, row:row + CASES, t * LANES:(t + 1) * LANES] = value


def lane_kernel(out):
    out[...] = iota((ROWS, LANES), 1)


def split_kernel(table, blocks, chip, own, loads, lanes, high, low, cells, start, info, load_cells):
    count = NNZ * 288
    for i in range(P_SIZE):
        put_cells(loads[i], load_cells, i)
        put_cells(chip[i], cells, i)
        put_cells(own[i], cells, P_SIZE + i)
    unit_row, unit_col = iota((PAIRS, 384), 0), iota((PAIRS, 384), 1)
    pair = (unit_row % 32) * 3 + unit_row // 32
    unit = one_hot((unit_col == 2 * pair) | (unit_col == 2 * pair + B + 1))
    for g in range(P_SIZE):
        start[g] = lax.dot_general(unit, load_cells[g], NT, preferred_element_type=F32)
        for j in range(NNZ):
            for t in range(3):
                tall = jnp.concatenate(
                    [blocks[pl.ds(g * count + 12 * k + j + 4 * t, 32, stride=36), :] for k in range(3)], axis=0)
                at = (g, slice(None), slice(j * 384 + t * LANES, j * 384 + (t + 1) * LANES))
                high[at], low[at] = halves(tall)

    lane = lanes[...]
    notes = jnp.zeros((ROWS, LANES), jnp.int32)
    for k in range(LEAF):
        for m in range(UPD):
            notes = jnp.where(lane == k * UPD + m, table[8 + k, m], notes)
    for i in range(P_SIZE):
        source = table[4, i]
        notes = jnp.where(lane == 64 + i, source // P_SIZE, notes)
        notes = jnp.where(lane == 76 + i, source % P_SIZE, notes)
    info[...] = notes.astype(F32)[:1]


def residual_kernel(table, high, low, near, start, info, far, out, cells, message):
    for i in range(P_SIZE):
        cells[i] = near[i]
        cells[P_SIZE + i] = near[P_SIZE + i]
        put_cells(far[i], cells, 2 * P_SIZE + i)

    residuals = ([], [])
    for g in range(P_SIZE):
        right = jnp.concatenate([cells[table[j, g]] for j in range(NNZ)], axis=1)
        total = start[g]
        for side in (high, low):
            total = total - lax.dot_general(side[g], right, NT, preferred_element_type=F32)
        for par in range(2):
            one = total[:, par * 32:par * 32 + 16] + total[:, par * 32 + 16:par * 32 + 32]
            residuals[par].append(one)

    squares = jnp.zeros((PAIRS, LANES), F32)
    for par in range(2):
        ones = residuals[par] + [jnp.zeros((PAIRS, CASES), F32)] * 4
        for t in range(2):
            tile = jnp.concatenate(ones[8 * t:8 * t + 8], axis=1)
            squares = squares + tile * tile
            for k in range(3):
                message[pl.ds(par * 256 + 2 * k + t, 32, stride=ROWS), :] = tile[k * 32:(k + 1) * 32]
    whole = jnp.sum(squares).reshape(1, 1)
    first = whole.astype(BF16).astype(F32)
    second = (whole - first).astype(BF16).astype(F32)
    third = whole - first - second
    lane = iota((DOM, LANES), 1)
    message[pl.ds(6, DOM, stride=ROWS), :] = jnp.broadcast_to(info[...], (DOM, LANES))
    message[pl.ds(7, DOM, stride=ROWS), :] = jnp.where(
        lane == 0, first, jnp.where(lane == 1, second, jnp.where(lane == 2, third, 0.0)))
    out[...] = message[...].astype(BF16)


def permute_kernel(received, out, notes, squares, wide, message):
    wide[...] = received[...].astype(F32)
    info = wide[pl.ds(6, DOM, stride=ROWS), :]
    notes[...] = info
    squares[...] = jnp.broadcast_to(jnp.sum(wide[pl.ds(7, DOM, stride=ROWS), :]).reshape(1, 1), (1, LANES))
    rows = jnp.concatenate(
        [wide[pl.ds(s, DOM, stride=ROWS), :].astype(BF16) for s in range(6)], axis=1)
    lane = iota((DOM, LANES), 1)
    source = iota((DOM, DOM), 1).astype(F32)
    place = (iota((DOM, 256), 1) // CASES).astype(F32)
    chosen, keep = [], []
    for i in range(P_SIZE):
        device = jnp.sum(jnp.where(lane == 64 + i, info, 0.0), axis=1, keepdims=True)
        row = jnp.sum(jnp.where(lane == 76 + i, info, 0.0), axis=1, keepdims=True)
        chosen.append(one_hot(device == source))
        keep.append(row == place)
    taken = dot(jnp.concatenate(chosen, axis=0), rows)
    fold = one_hot(iota((256, LANES), 0) % CASES == iota((256, LANES), 1) % CASES)
    for k in range(3):
        kept = jnp.concatenate(
            [jnp.where(keep[i], taken[i * DOM:(i + 1) * DOM, k * 256:(k + 1) * 256], 0.0).astype(BF16)
             for i in range(P_SIZE)], axis=0)
        copies = dot(kept, fold)
        for t, count in ((0, LEAF), (1, ANC)):
            moved = jnp.zeros((DOM, LANES), F32)
            for i in range(count):
                at = (LEAF * t + i) * DOM
                moved = jnp.where(lane // CASES == i, copies[at:at + DOM], moved)
            message[pl.ds(2 * k + t, DOM, stride=ROWS), :] = moved
    for s in (6, 7):
        message[pl.ds(s, DOM, stride=ROWS), :] = jnp.zeros((DOM, LANES), F32)
    out[...] = message[...].astype(BF16)


def update_kernel(received, inverses, tiles, squares, level, ancestors, out, squares_out,
                  wide, leaf, rest, right, near, sems, partial):
    copies = [pltpu.make_async_copy(tiles.at[pl.ds(k * PAIRS, PAIRS)], near.at[pl.ds(k * PAIRS, PAIRS)],
                                    sems.at[k]) for k in range(LEAF)]
    for copy in copies:
        copy.start()
    squares_out[...] = squares[...]
    wide[...] = received[...].astype(F32)
    for k in range(3):
        for par in range(2):
            at = pl.ds(2 * k + par, 32, stride=6)
            leaf[at, :] = wide[pl.ds(par * 256 + 2 * k, 32, stride=ROWS), :]
            rest[at, :] = wide[pl.ds(par * 256 + 2 * k + 1, 32, stride=ROWS), :]

    def doubled(x):
        zeros = jnp.zeros_like(x)
        return jnp.concatenate(
            [jnp.concatenate([x, zeros], axis=1), jnp.concatenate([zeros, x], axis=1)], axis=0)

    def left(ref, start, count):
        return jnp.concatenate(
            [ref[pl.ds(start, count), t].reshape(count * 8, LANES) for t in range(3)], axis=1)

    solved = dot(left(inverses, 0, PAIRS), doubled(leaf[...].astype(BF16)))
    own = iota((768, 256), 0) % 8 == (iota((768, 256), 1) % LANES) // 16
    solved = jnp.where(own, solved, 0.0).astype(BF16)
    gather = one_hot(iota((B, 768), 1) // 8 == iota((B, 768), 0) // 2)
    solved = dot(gather, solved)
    solved = jnp.where(iota((B, LANES), 0) % 2 == 0, solved[:, :LANES], solved[:, LANES:])
    unit = one_hot(iota((LANES, LANES), 0) == iota((LANES, LANES), 1))
    level[...] = lax.dot_general(unit, solved.astype(BF16), NT, preferred_element_type=F32).astype(BF16)
    ancestors[...] = lax.dot_general(
        unit[:64], rest[...].astype(BF16), NT, preferred_element_type=F32)
    owner = iota((B, LANES), 1) // 16
    for k in range(LEAF):
        right[k * 384:(k + 1) * 384] = doubled(jnp.where(owner == k, solved, 0.0)).astype(BF16)
    step, band = LEAF // 2, PAIRS // 2
    for first in range(0, LEAF, step):
        for copy in copies[first:first + step]:
            copy.wait()
        for r in range(0, PAIRS, band):
            at = slice(r * 8, (r + band) * 8)
            wide_left = jnp.concatenate(
                [left(near, k * PAIRS + r, band) for k in range(first, first + step)], axis=1)
            total = dot(wide_left, right[first * 384:(first + step) * 384])
            if first == 0:
                partial[at] = total
            else:
                out[at] = (partial[at] + total).astype(BF16)


def sum_kernel(received, targets, squares, out, squares_out, right):
    squares_out[...] = squares[...]
    select = one_hot(targets[...] == iota((256, 512), 0).astype(F32))
    group = iota((64, LANES), 1) // CASES
    for tile in range(3):
        parts = []
        for pair in range(tile * 4, tile * 4 + 4):
            rows = jnp.concatenate(
                [received[s, pair * 8:(pair + 1) * 8, :].astype(F32) for s in range(GROUP)], axis=0)
            parts.extend([rows[:, :LANES], rows[:, LANES:]])
        for step in (4, 2, 1):
            upper = (group // step) % 2 == 1
            turned = list(parts)
            for i in range(8):
                if not i & step:
                    a, b = parts[i], parts[i + step]
                    turned[i] = jnp.where(upper, pltpu.roll(b, step * CASES, 1), a)
                    turned[i + step] = jnp.where(upper, b, pltpu.roll(a, LANES - step * CASES, 1))
            parts = turned
        for k in range(LEAF):
            right[k * 64:(k + 1) * 64, tile * LANES:(tile + 1) * LANES] = parts[k].astype(BF16)
    out[...] = dot(select, right[...]).reshape(DOM, ANC, 384).astype(BF16)


def final_kernel(received, ancestors, out):
    place = iota((32, 256), 1)
    source, block = place // ANC, place % ANC
    group = source // (N_Z * N_CORE) * N_CORE + source % N_CORE
    row = iota((32, 256), 0)
    pick = one_hot((row % ANC == block) & (row // ANC == group))
    summed = dot(pick, received[...])
    count = ANC * CASES
    own = iota((count, 384), 1) % CASES == iota((count, 384), 0) % CASES
    sides = ([], [])
    for q in range(GROUP):
        left = jnp.concatenate(
            [jnp.broadcast_to(summed[q * ANC + t:q * ANC + t + 1], (CASES, 384)) for t in range(ANC)], axis=0)
        for side, part in zip(sides, halves(jnp.where(own, left, 0.0))):
            side.append(part)
    column = one_hot(iota((384, 24), 1) == iota((384, 24), 0) // CASES)
    both = dot(jnp.concatenate(sides[0] + sides[1], axis=0), column)
    both = both[:GROUP * count] + both[GROUP * count:]
    out[...] = ancestors[...] - jnp.concatenate(
        [both[q * count:(q + 1) * count] for q in range(GROUP)], axis=1)


def call(kernel, name, shapes, in_specs, scratch, megabytes=16, cost=None):
    outs = [jax.ShapeDtypeStruct(*s) for s in shapes]
    return pl.pallas_call(
        kernel,
        out_shape=outs,
        in_specs=in_specs,
        out_specs=[pl.BlockSpec(memory_space=pltpu.VMEM)] * len(outs),
        scratch_shapes=scratch,
        compiler_params=pltpu.CompilerParams(vmem_limit_bytes=megabytes * 2**20),
        cost_estimate=cost,
        name=name,
    )


def on_device(solution, loads, blocks, columns, row_source, inverses, tiles, targets):
    vmem = pl.BlockSpec(memory_space=pltpu.VMEM)
    smem = pl.BlockSpec(memory_space=pltpu.SMEM)
    hbm = pl.BlockSpec(memory_space=pltpu.HBM)
    dma = pltpu.SemaphoreType.DMA
    device = lax.axis_index("dom")
    far = lax.ppermute(solution, "dom", [(i, i + 1 if i % 2 else i - 1) for i in range(1, DOM - 1)])
    chip = lax.ppermute(solution, "dom", [(i, i ^ 1) for i in range(DOM)])
    local = columns.T - (device * P_SIZE - P_SIZE)
    turn = jnp.where(local < P_SIZE, 2 * P_SIZE, jnp.where(local < 2 * P_SIZE, 0, -2 * P_SIZE))
    local = local + jnp.where(device % 2 == 0, turn, 0)
    table = jnp.concatenate([
        jnp.pad(local, ((0, 0), (0, LANES - P_SIZE))),
        jnp.pad(row_source.reshape(1, P_SIZE), ((0, 3), (0, LANES - P_SIZE))),
        jnp.pad(targets, ((0, 0), (0, LANES - UPD)))], axis=0)
    natural = blocks.reshape(P_SIZE, NNZ, 288, LANES).transpose(0, 2, 1, 3).reshape(P_SIZE * 1152, LANES)
    natural_inverses = inverses.reshape(LEAF, 288, LANES).transpose(1, 0, 2).reshape(PAIRS, 3, LEAF, LANES)
    natural_tiles = tiles.reshape(LEAF, UPD, 288, LANES).transpose(0, 2, 1, 3)
    natural_tiles = natural_tiles.reshape(LEAF * PAIRS, 3, UPD, LANES)
    (lanes,) = call(
        lane_kernel, "lanes", [((ROWS, LANES), jnp.int32)], [], [], 16,
        pl.CostEstimate(flops=3 * 10**10, bytes_accessed=10**6, transcendentals=0))()
    high, low, cells, start, info = call(
        split_kernel, "split",
        [((P_SIZE, PAIRS, 1536), BF16), ((P_SIZE, PAIRS, 1536), BF16), ((2 * P_SIZE, 64, 384), BF16),
         ((P_SIZE, PAIRS, 64), F32), ((1, LANES), F32)],
        [smem] + [vmem] * 5, [pltpu.VMEM((P_SIZE, 64, 384), BF16)], 16,
        pl.CostEstimate(flops=10**9, bytes_accessed=14 * 10**6, transcendentals=0),
    )(table, natural, chip, solution, loads, lanes)
    (message,) = call(
        residual_kernel, "residual", [((DOM * ROWS, LANES), BF16)],
        [smem] + [vmem] * 6,
        [pltpu.VMEM((3 * P_SIZE, 64, 384), BF16), pltpu.VMEM((DOM * ROWS, LANES), F32)], 16,
    )(table, high, low, cells, start, info, far)

    def exchange(x):
        x = x.reshape(DOM, ROWS, LANES)
        return lax.all_to_all(x, "dom", 0, 0, tiled=True).reshape(DOM * ROWS, LANES)

    def across(x, step):
        return x + lax.ppermute(x, "rhs", [(i, i ^ step) for i in range(4)])

    message, notes, squares = call(
        permute_kernel, "permute",
        [((DOM * ROWS, LANES), BF16), ((DOM, LANES), F32), ((1, LANES), F32)], [vmem],
        [pltpu.VMEM((DOM * ROWS, LANES), F32), pltpu.VMEM((DOM * ROWS, LANES), F32)], 16,
        pl.CostEstimate(flops=4 * 10**9, bytes_accessed=10**6, transcendentals=0),
    )(exchange(message))

    level, ancestors, message, squares = call(
        update_kernel, "update",
        [((LEAF * CASES, B), BF16), ((ANC * CASES, B), F32), ((PAIRS * UPD, 256), BF16), ((1, LANES), F32)],
        [vmem, vmem, hbm, vmem],
        [pltpu.VMEM((DOM * ROWS, LANES), F32), pltpu.VMEM((B, LANES), F32), pltpu.VMEM((B, LANES), F32),
         pltpu.VMEM((LEAF * 384, 256), BF16), pltpu.VMEM((LEAF * PAIRS, 3, UPD, LANES), BF16),
         dma((LEAF,)), pltpu.VMEM((PAIRS * UPD, 256), F32)], 52,
    )(exchange(message), natural_inverses, natural_tiles, across(squares, 1))

    groups = [[(x * N_Z + z) * N_CORE + c for x in range(N_X) for c in range(N_CORE)] for z in range(N_Z)]
    received = lax.all_to_all(
        message.reshape(GROUP, 96, 256), "dom", 0, 0, axis_index_groups=groups, tiled=True)
    z = (device // N_CORE) % N_Z
    near = lax.dynamic_index_in_dim(notes.reshape(N_X, N_Z, N_CORE, LANES), z, axis=1, keepdims=False)
    near = near.reshape(GROUP, LANES)[:, :LEAF * UPD].reshape(GROUP, LEAF, UPD)
    near = near.transpose(1, 0, 2).reshape(1, LEAF * GROUP * UPD)
    sums, squares = call(
        sum_kernel, "sum", [((DOM, ANC, 384), BF16), ((1, LANES), F32)], [vmem] * 3,
        [pltpu.VMEM((512, 384), BF16)],
    )(received, near, across(squares, 2))
    residual_rms = jnp.sqrt(squares[0, 0] / (DOM * P_SIZE * CASES * 4 * B))
    sums = lax.all_to_all(sums, "dom", 0, 0, tiled=True)
    (ancestor_rhs,) = call(final_kernel, "final", [((ANC * CASES, B), F32)], [vmem] * 2, [])(
        sums.reshape(DOM * ANC, 384), ancestors)
    return (level.reshape(LEAF, CASES, B), ancestor_rhs.reshape(ANC, CASES, B), residual_rms)


def solution(mesh):
    placed = (
        P("dom", "rhs", None),
        P("dom", "rhs", None),
        P("dom", None, None),
        P("dom", None),
        P("dom"),
        P("dom", None),
        P("dom", None, None),
        P("dom", None),
    )
    return jax.shard_map(
        on_device,
        mesh=mesh,
        in_specs=placed,
        out_specs=(P("dom", "rhs", None), P("dom", "rhs", None), P()),
        check_vma=False,
    )
```

```python
import jax
import jax.numpy as jnp
from jax import lax
from jax.experimental import pallas as pl
from jax.experimental.pallas import tpu as pltpu
from jax.sharding import PartitionSpec as P

B = 192
LEAF = 8
ANC = 4
NNZ = 4
UPD = 8
P_SIZE = 12
CASES = 16
DOM = 64
N_X, N_Z, N_CORE = 4, 8, 2
GROUP = N_X * N_CORE
LANES = 128
ROWS = 8
PAIRS = B // 2
BF16 = jnp.bfloat16
F32 = jnp.float32
NT = (((1,), (1,)), ((), ()))


def iota(shape, dim):
    return lax.broadcasted_iota(jnp.int32, shape, dim)


def one_hot(condition):
    return jnp.where(condition, 1.0, 0.0).astype(BF16)


def halves(x):
    high = x.astype(BF16)
    return high, (x - high.astype(F32)).astype(BF16)


def dot(a, b):
    return jnp.dot(a, b, preferred_element_type=F32)


def put_cells(x, cells, slot):
    wide, narrow = x[:, :LANES], jnp.concatenate([x[:, LANES:], jnp.zeros((CASES, 64), F32)], axis=1)
    lower = iota((CASES, LANES), 1) < 64
    zeros = jnp.zeros((CASES, LANES), F32)
    turned = pltpu.roll(wide, 64, 1)
    lines = (
        (wide, narrow, zeros),
        (zeros, jnp.where(lower, 0.0, turned), jnp.where(lower, turned, pltpu.roll(narrow, 64, 1))),
    )
    for par in range(2):
        for t in range(3):
            for part, value in enumerate(halves(lines[par][t])):
                row = (2 * par + part) * CASES
                cells[slot, row:row + CASES, t * LANES:(t + 1) * LANES] = value


def lane_kernel(out):
    out[...] = iota((ROWS, LANES), 1)


def split_kernel(table, blocks, chip, own, loads, lanes, high, low, cells, start, info,
                 load_cells, wide, sems):
    count = NNZ * 288
    copies = [pltpu.make_async_copy(blocks.at[pl.ds(g * count, count)], wide.at[pl.ds(g * count, count)],
                                    sems.at[g]) for g in range(P_SIZE)]
    for copy in copies:
        copy.start()
    for i in range(P_SIZE):
        put_cells(loads[i], load_cells, i)
        put_cells(chip[i], cells, i)
        put_cells(own[i], cells, P_SIZE + i)
    unit_row, unit_col = iota((PAIRS, 384), 0), iota((PAIRS, 384), 1)
    pair = (unit_row % 32) * 3 + unit_row // 32
    unit = one_hot((unit_col == 2 * pair) | (unit_col == 2 * pair + B + 1))
    for g in range(P_SIZE):
        start[g] = lax.dot_general(unit, load_cells[g], NT, preferred_element_type=F32)
    lane = lanes[...]
    notes = jnp.zeros((ROWS, LANES), jnp.int32)
    for k in range(LEAF):
        for m in range(UPD):
            notes = jnp.where(lane == k * UPD + m, table[8 + k, m], notes)
    for i in range(P_SIZE):
        source = table[4, i]
        notes = jnp.where(lane == 64 + i, source // P_SIZE, notes)
        notes = jnp.where(lane == 76 + i, source % P_SIZE, notes)
    info[...] = notes.astype(F32)[:1]

    for g in range(P_SIZE):
        if g % 2 == 0:
            for copy in copies[g:g + 2]:
                copy.wait()
        for j in range(NNZ):
            for t in range(3):
                tall = jnp.concatenate(
                    [wide[pl.ds(g * count + 12 * k + j + 4 * t, 32, stride=36), :] for k in range(3)], axis=0)
                at = (g, slice(None), slice(j * 384 + t * LANES, j * 384 + (t + 1) * LANES))
                high[at], low[at] = halves(tall)


def residual_kernel(table, high, low, near, start, info, far, out, cells, message):
    for i in range(P_SIZE):
        cells[i] = near[i]
        cells[P_SIZE + i] = near[P_SIZE + i]
        put_cells(far[i], cells, 2 * P_SIZE + i)

    residuals = ([], [])
    for g in range(P_SIZE):
        right = jnp.concatenate([cells[table[j, g]] for j in range(NNZ)], axis=1)
        total = start[g]
        for side in (high, low):
            total = total - lax.dot_general(side[g], right, NT, preferred_element_type=F32)
        for par in range(2):
            one = total[:, par * 32:par * 32 + 16] + total[:, par * 32 + 16:par * 32 + 32]
            residuals[par].append(one)

    squares = jnp.zeros((PAIRS, LANES), F32)
    for par in range(2):
        ones = residuals[par] + [jnp.zeros((PAIRS, CASES), F32)] * 4
        for t in range(2):
            tile = jnp.concatenate(ones[8 * t:8 * t + 8], axis=1)
            squares = squares + tile * tile
            for k in range(3):
                message[pl.ds(par * 256 + 2 * k + t, 32, stride=ROWS), :] = tile[k * 32:(k + 1) * 32]
    whole = jnp.sum(squares).reshape(1, 1)
    first = whole.astype(BF16).astype(F32)
    second = (whole - first).astype(BF16).astype(F32)
    third = whole - first - second
    lane = iota((DOM, LANES), 1)
    message[pl.ds(6, DOM, stride=ROWS), :] = jnp.broadcast_to(info[...], (DOM, LANES))
    message[pl.ds(7, DOM, stride=ROWS), :] = jnp.where(
        lane == 0, first, jnp.where(lane == 1, second, jnp.where(lane == 2, third, 0.0)))
    out[...] = message[...].astype(BF16)


def permute_kernel(received, out, notes, squares, wide, message):
    wide[...] = received[...].astype(F32)
    info = wide[pl.ds(6, DOM, stride=ROWS), :]
    notes[...] = info
    squares[...] = jnp.broadcast_to(jnp.sum(wide[pl.ds(7, DOM, stride=ROWS), :]).reshape(1, 1), (1, LANES))
    rows = jnp.concatenate(
        [wide[pl.ds(s, DOM, stride=ROWS), :].astype(BF16) for s in range(6)], axis=1)
    lane = iota((DOM, LANES), 1)
    source = iota((DOM, DOM), 1).astype(F32)
    place = (iota((DOM, 256), 1) // CASES).astype(F32)
    chosen, keep = [], []
    for i in range(P_SIZE):
        device = jnp.sum(jnp.where(lane == 64 + i, info, 0.0), axis=1, keepdims=True)
        row = jnp.sum(jnp.where(lane == 76 + i, info, 0.0), axis=1, keepdims=True)
        chosen.append(one_hot(device == source))
        keep.append(row == place)
    taken = dot(jnp.concatenate(chosen, axis=0), rows)
    fold = one_hot(iota((256, LANES), 0) % CASES == iota((256, LANES), 1) % CASES)
    for k in range(3):
        kept = jnp.concatenate(
            [jnp.where(keep[i], taken[i * DOM:(i + 1) * DOM, k * 256:(k + 1) * 256], 0.0).astype(BF16)
             for i in range(P_SIZE)], axis=0)
        copies = dot(kept, fold)
        for t, count in ((0, LEAF), (1, ANC)):
            moved = jnp.zeros((DOM, LANES), F32)
            for i in range(count):
                at = (LEAF * t + i) * DOM
                moved = jnp.where(lane // CASES == i, copies[at:at + DOM], moved)
            message[pl.ds(2 * k + t, DOM, stride=ROWS), :] = moved
    for s in (6, 7):
        message[pl.ds(s, DOM, stride=ROWS), :] = jnp.zeros((DOM, LANES), F32)
    out[...] = message[...].astype(BF16)


def update_kernel(received, inverses, tiles, squares, level, ancestors, out, squares_out,
                  wide, leaf, rest, right, near, sems, partial):
    copies = [pltpu.make_async_copy(tiles.at[pl.ds(k * PAIRS, PAIRS)], near.at[pl.ds(k * PAIRS, PAIRS)],
                                    sems.at[k]) for k in range(LEAF)]
    for copy in copies:
        copy.start()
    squares_out[...] = squares[...]
    wide[...] = received[...].astype(F32)
    for k in range(3):
        for par in range(2):
            at = pl.ds(2 * k + par, 32, stride=6)
            leaf[at, :] = wide[pl.ds(par * 256 + 2 * k, 32, stride=ROWS), :]
            rest[at, :] = wide[pl.ds(par * 256 + 2 * k + 1, 32, stride=ROWS), :]

    def doubled(x):
        zeros = jnp.zeros_like(x)
        return jnp.concatenate(
            [jnp.concatenate([x, zeros], axis=1), jnp.concatenate([zeros, x], axis=1)], axis=0)

    def left(ref, start, count):
        return jnp.concatenate(
            [ref[pl.ds(start, count), t].reshape(count * 8, LANES) for t in range(3)], axis=1)

    solved = dot(left(inverses, 0, PAIRS), doubled(leaf[...].astype(BF16)))
    own = iota((768, 256), 0) % 8 == (iota((768, 256), 1) % LANES) // 16
    solved = jnp.where(own, solved, 0.0).astype(BF16)
    gather = one_hot(iota((B, 768), 1) // 8 == iota((B, 768), 0) // 2)
    solved = dot(gather, solved)
    solved = jnp.where(iota((B, LANES), 0) % 2 == 0, solved[:, :LANES], solved[:, LANES:])
    unit = one_hot(iota((LANES, LANES), 0) == iota((LANES, LANES), 1))
    level[...] = lax.dot_general(unit, solved.astype(BF16), NT, preferred_element_type=F32).astype(BF16)
    ancestors[...] = lax.dot_general(
        unit[:64], rest[...].astype(BF16), NT, preferred_element_type=F32)
    owner = iota((B, LANES), 1) // 16
    for k in range(LEAF):
        right[k * 384:(k + 1) * 384] = doubled(jnp.where(owner == k, solved, 0.0)).astype(BF16)
    step, band = LEAF // 2, PAIRS // 2
    for first in range(0, LEAF, step):
        for copy in copies[first:first + step]:
            copy.wait()
        for r in range(0, PAIRS, band):
            at = slice(r * 8, (r + band) * 8)
            wide_left = jnp.concatenate(
                [left(near, k * PAIRS + r, band) for k in range(first, first + step)], axis=1)
            total = dot(wide_left, right[first * 384:(first + step) * 384])
            if first == 0:
                partial[at] = total
            else:
                out[at] = (partial[at] + total).astype(BF16)


def sum_kernel(received, targets, squares, out, squares_out, right):
    squares_out[...] = squares[...]
    select = one_hot(targets[...] == iota((256, 512), 0).astype(F32))
    group = iota((64, LANES), 1) // CASES
    for tile in range(3):
        parts = []
        for pair in range(tile * 4, tile * 4 + 4):
            rows = jnp.concatenate(
                [received[s, pair * 8:(pair + 1) * 8, :].astype(F32) for s in range(GROUP)], axis=0)
            parts.extend([rows[:, :LANES], rows[:, LANES:]])
        for step in (4, 2, 1):
            upper = (group // step) % 2 == 1
            turned = list(parts)
            for i in range(8):
                if not i & step:
                    a, b = parts[i], parts[i + step]
                    turned[i] = jnp.where(upper, pltpu.roll(b, step * CASES, 1), a)
                    turned[i + step] = jnp.where(upper, b, pltpu.roll(a, LANES - step * CASES, 1))
            parts = turned
        for k in range(LEAF):
            right[k * 64:(k + 1) * 64, tile * LANES:(tile + 1) * LANES] = parts[k].astype(BF16)
    out[...] = dot(select, right[...]).reshape(DOM, ANC, 384).astype(BF16)


def final_kernel(received, ancestors, out):
    place = iota((32, 256), 1)
    source, block = place // ANC, place % ANC
    group = source // (N_Z * N_CORE) * N_CORE + source % N_CORE
    row = iota((32, 256), 0)
    pick = one_hot((row % ANC == block) & (row // ANC == group))
    summed = dot(pick, received[...])
    count = ANC * CASES
    own = iota((count, 384), 1) % CASES == iota((count, 384), 0) % CASES
    sides = ([], [])
    for q in range(GROUP):
        left = jnp.concatenate(
            [jnp.broadcast_to(summed[q * ANC + t:q * ANC + t + 1], (CASES, 384)) for t in range(ANC)], axis=0)
        for side, part in zip(sides, halves(jnp.where(own, left, 0.0))):
            side.append(part)
    column = one_hot(iota((384, 24), 1) == iota((384, 24), 0) // CASES)
    both = dot(jnp.concatenate(sides[0] + sides[1], axis=0), column)
    both = both[:GROUP * count] + both[GROUP * count:]
    out[...] = ancestors[...] - jnp.concatenate(
        [both[q * count:(q + 1) * count] for q in range(GROUP)], axis=1)


def call(kernel, name, shapes, in_specs, scratch, megabytes=16, cost=None):
    outs = [jax.ShapeDtypeStruct(*s) for s in shapes]
    return pl.pallas_call(
        kernel,
        out_shape=outs,
        in_specs=in_specs,
        out_specs=[pl.BlockSpec(memory_space=pltpu.VMEM)] * len(outs),
        scratch_shapes=scratch,
        compiler_params=pltpu.CompilerParams(vmem_limit_bytes=megabytes * 2**20),
        cost_estimate=cost,
        name=name,
    )


def on_device(solution, loads, blocks, columns, row_source, inverses, tiles, targets):
    vmem = pl.BlockSpec(memory_space=pltpu.VMEM)
    smem = pl.BlockSpec(memory_space=pltpu.SMEM)
    hbm = pl.BlockSpec(memory_space=pltpu.HBM)
    dma = pltpu.SemaphoreType.DMA
    device = lax.axis_index("dom")
    far = lax.ppermute(solution, "dom", [(i, i + 1 if i % 2 else i - 1) for i in range(1, DOM - 1)])
    chip = lax.ppermute(solution, "dom", [(i, i ^ 1) for i in range(DOM)])
    local = columns.T - (device * P_SIZE - P_SIZE)
    turn = jnp.where(local < P_SIZE, 2 * P_SIZE, jnp.where(local < 2 * P_SIZE, 0, -2 * P_SIZE))
    local = local + jnp.where(device % 2 == 0, turn, 0)
    table = jnp.concatenate([
        jnp.pad(local, ((0, 0), (0, LANES - P_SIZE))),
        jnp.pad(row_source.reshape(1, P_SIZE), ((0, 3), (0, LANES - P_SIZE))),
        jnp.pad(targets, ((0, 0), (0, LANES - UPD)))], axis=0)
    natural = blocks.reshape(P_SIZE, NNZ, 288, LANES).transpose(0, 2, 1, 3).reshape(P_SIZE * 1152, LANES)
    natural_inverses = inverses.reshape(LEAF, 288, LANES).transpose(1, 0, 2).reshape(PAIRS, 3, LEAF, LANES)
    natural_tiles = tiles.reshape(LEAF, UPD, 288, LANES).transpose(0, 2, 1, 3)
    natural_tiles = natural_tiles.reshape(LEAF * PAIRS, 3, UPD, LANES)
    (lanes,) = call(
        lane_kernel, "lanes", [((ROWS, LANES), jnp.int32)], [], [], 16,
        pl.CostEstimate(flops=3 * 10**10, bytes_accessed=10**6, transcendentals=0))()
    high, low, cells, start, info = call(
        split_kernel, "split",
        [((P_SIZE, PAIRS, 1536), BF16), ((P_SIZE, PAIRS, 1536), BF16), ((2 * P_SIZE, 64, 384), BF16),
         ((P_SIZE, PAIRS, 64), F32), ((1, LANES), F32)],
        [smem, hbm] + [vmem] * 4,
        [pltpu.VMEM((P_SIZE, 64, 384), BF16), pltpu.VMEM((P_SIZE * 1152, LANES), F32), dma((P_SIZE,))], 41,
        pl.CostEstimate(flops=10**9, bytes_accessed=14 * 10**6, transcendentals=0),
    )(table, natural, chip, solution, loads, lanes)
    (message,) = call(
        residual_kernel, "residual", [((DOM * ROWS, LANES), BF16)],
        [smem] + [vmem] * 6,
        [pltpu.VMEM((3 * P_SIZE, 64, 384), BF16), pltpu.VMEM((DOM * ROWS, LANES), F32)], 16,
    )(table, high, low, cells, start, info, far)

    def exchange(x):
        x = x.reshape(DOM, ROWS, LANES)
        return lax.all_to_all(x, "dom", 0, 0, tiled=True).reshape(DOM * ROWS, LANES)

    def across(x, step):
        return x + lax.ppermute(x, "rhs", [(i, i ^ step) for i in range(4)])

    message, notes, squares = call(
        permute_kernel, "permute",
        [((DOM * ROWS, LANES), BF16), ((DOM, LANES), F32), ((1, LANES), F32)], [vmem],
        [pltpu.VMEM((DOM * ROWS, LANES), F32), pltpu.VMEM((DOM * ROWS, LANES), F32)], 16,
        pl.CostEstimate(flops=4 * 10**9, bytes_accessed=10**6, transcendentals=0),
    )(exchange(message))

    level, ancestors, message, squares = call(
        update_kernel, "update",
        [((LEAF * CASES, B), BF16), ((ANC * CASES, B), F32), ((PAIRS * UPD, 256), BF16), ((1, LANES), F32)],
        [vmem, vmem, hbm, vmem],
        [pltpu.VMEM((DOM * ROWS, LANES), F32), pltpu.VMEM((B, LANES), F32), pltpu.VMEM((B, LANES), F32),
         pltpu.VMEM((LEAF * 384, 256), BF16), pltpu.VMEM((LEAF * PAIRS, 3, UPD, LANES), BF16),
         dma((LEAF,)), pltpu.VMEM((PAIRS * UPD, 256), F32)], 52,
    )(exchange(message), natural_inverses, natural_tiles, across(squares, 1))

    groups = [[(x * N_Z + z) * N_CORE + c for x in range(N_X) for c in range(N_CORE)] for z in range(N_Z)]
    received = lax.all_to_all(
        message.reshape(GROUP, 96, 256), "dom", 0, 0, axis_index_groups=groups, tiled=True)
    z = (device // N_CORE) % N_Z
    near = lax.dynamic_index_in_dim(notes.reshape(N_X, N_Z, N_CORE, LANES), z, axis=1, keepdims=False)
    near = near.reshape(GROUP, LANES)[:, :LEAF * UPD].reshape(GROUP, LEAF, UPD)
    near = near.transpose(1, 0, 2).reshape(1, LEAF * GROUP * UPD)
    sums, squares = call(
        sum_kernel, "sum", [((DOM, ANC, 384), BF16), ((1, LANES), F32)], [vmem] * 3,
        [pltpu.VMEM((512, 384), BF16)],
    )(received, near, across(squares, 2))
    residual_rms = jnp.sqrt(squares[0, 0] / (DOM * P_SIZE * CASES * 4 * B))
    sums = lax.all_to_all(sums, "dom", 0, 0, tiled=True)
    (ancestor_rhs,) = call(final_kernel, "final", [((ANC * CASES, B), F32)], [vmem] * 2, [])(
        sums.reshape(DOM * ANC, 384), ancestors)
    return (level.reshape(LEAF, CASES, B), ancestor_rhs.reshape(ANC, CASES, B), residual_rms)


def solution(mesh):
    placed = (
        P("dom", "rhs", None),
        P("dom", "rhs", None),
        P("dom", None, None),
        P("dom", None),
        P("dom"),
        P("dom", None),
        P("dom", None, None),
        P("dom", None),
    )
    return jax.shard_map(
        on_device,
        mesh=mesh,
        in_specs=placed,
        out_specs=(P("dom", "rhs", None), P("dom", "rhs", None), P()),
        check_vma=False,
    )
```

```python
import jax
import jax.numpy as jnp
from jax import lax
from jax.experimental import pallas as pl
from jax.experimental.pallas import tpu as pltpu
from jax.sharding import PartitionSpec as P

B = 192
LEAF = 8
ANC = 4
NNZ = 4
UPD = 8
P_SIZE = 12
CASES = 16
DOM = 64
N_X, N_Z, N_CORE = 4, 8, 2
GROUP = N_X * N_CORE
LANES = 128
ROWS = 8
PAIRS = B // 2
BF16 = jnp.bfloat16
F32 = jnp.float32
NT = (((1,), (1,)), ((), ()))


def iota(shape, dim):
    return lax.broadcasted_iota(jnp.int32, shape, dim)


def one_hot(condition):
    return jnp.where(condition, 1.0, 0.0).astype(BF16)


def halves(x):
    high = x.astype(BF16)
    return high, (x - high.astype(F32)).astype(BF16)


def dot(a, b):
    return jnp.dot(a, b, preferred_element_type=F32)


def put_cells(x, cells, slot):
    wide, narrow = x[:, :LANES], jnp.concatenate([x[:, LANES:], jnp.zeros((CASES, 64), F32)], axis=1)
    lower = iota((CASES, LANES), 1) < 64
    zeros = jnp.zeros((CASES, LANES), F32)
    turned = pltpu.roll(wide, 64, 1)
    lines = (
        (wide, narrow, zeros),
        (zeros, jnp.where(lower, 0.0, turned), jnp.where(lower, turned, pltpu.roll(narrow, 64, 1))),
    )
    for par in range(2):
        for t in range(3):
            for part, value in enumerate(halves(lines[par][t])):
                row = (2 * par + part) * CASES
                cells[slot, row:row + CASES, t * LANES:(t + 1) * LANES] = value


def lane_kernel(out):
    out[...] = iota((ROWS, LANES), 1)


def split_kernel(table, blocks, chip, own, loads, lanes, high, low, cells, start, info,
                 load_cells, wide, sems):
    count = NNZ * 288
    copies = [pltpu.make_async_copy(blocks.at[pl.ds(g * count, count)], wide.at[pl.ds(g * count, count)],
                                    sems.at[g]) for g in range(P_SIZE)]
    for copy in copies:
        copy.start()
    for i in range(P_SIZE):
        put_cells(loads[i], load_cells, i)
        put_cells(chip[i], cells, i)
        put_cells(own[i], cells, P_SIZE + i)
    unit_row, unit_col = iota((PAIRS, 384), 0), iota((PAIRS, 384), 1)
    pair = (unit_row % 32) * 3 + unit_row // 32
    unit = one_hot((unit_col == 2 * pair) | (unit_col == 2 * pair + B + 1))
    for g in range(P_SIZE):
        start[g] = lax.dot_general(unit, load_cells[g], NT, preferred_element_type=F32)
    lane = lanes[...]
    notes = jnp.zeros((ROWS, LANES), jnp.int32)
    for k in range(LEAF):
        for m in range(UPD):
            notes = jnp.where(lane == k * UPD + m, table[8 + k, m], notes)
    for i in range(P_SIZE):
        source = table[4, i]
        notes = jnp.where(lane == 64 + i, source // P_SIZE, notes)
        notes = jnp.where(lane == 76 + i, source % P_SIZE, notes)
    info[...] = notes.astype(F32)[:1]

    for g in range(P_SIZE):
        if g % 2 == 0:
            for copy in copies[g:g + 2]:
                copy.wait()
        for j in range(NNZ):
            for t in range(3):
                tall = jnp.concatenate(
                    [wide[pl.ds(g * count + 12 * k + j + 4 * t, 32, stride=36), :] for k in range(3)], axis=0)
                at = (g, slice(None), slice(j * 384 + t * LANES, j * 384 + (t + 1) * LANES))
                high[at], low[at] = halves(tall)


def residual_kernel(table, high, low, near, start, info, far, out, cells, message):
    for i in range(P_SIZE):
        cells[i] = near[i]
        cells[P_SIZE + i] = near[P_SIZE + i]
        put_cells(far[i], cells, 2 * P_SIZE + i)

    residuals = ([], [])
    for g in range(P_SIZE):
        right = jnp.concatenate([cells[table[j, g]] for j in range(NNZ)], axis=1)
        total = start[g]
        for side in (high, low):
            total = total - lax.dot_general(side[g], right, NT, preferred_element_type=F32)
        for par in range(2):
            one = total[:, par * 32:par * 32 + 16] + total[:, par * 32 + 16:par * 32 + 32]
            residuals[par].append(one)

    squares = jnp.zeros((PAIRS, LANES), F32)
    for par in range(2):
        ones = residuals[par] + [jnp.zeros((PAIRS, CASES), F32)] * 4
        for t in range(2):
            tile = jnp.concatenate(ones[8 * t:8 * t + 8], axis=1)
            squares = squares + tile * tile
            for k in range(3):
                message[pl.ds(par * 256 + 2 * k + t, 32, stride=ROWS), :] = tile[k * 32:(k + 1) * 32]
    whole = jnp.sum(squares).reshape(1, 1)
    first = whole.astype(BF16).astype(F32)
    second = (whole - first).astype(BF16).astype(F32)
    third = whole - first - second
    lane = iota((DOM, LANES), 1)
    message[pl.ds(6, DOM, stride=ROWS), :] = jnp.broadcast_to(info[...], (DOM, LANES))
    message[pl.ds(7, DOM, stride=ROWS), :] = jnp.where(
        lane == 0, first, jnp.where(lane == 1, second, jnp.where(lane == 2, third, 0.0)))
    out[...] = message[...].astype(BF16)


def permute_kernel(received, out, notes, squares, wide, message):
    wide[...] = received[...].astype(F32)
    info = wide[pl.ds(6, DOM, stride=ROWS), :]
    notes[...] = info
    squares[...] = jnp.broadcast_to(jnp.sum(wide[pl.ds(7, DOM, stride=ROWS), :]).reshape(1, 1), (1, LANES))
    rows = jnp.concatenate(
        [wide[pl.ds(s, DOM, stride=ROWS), :].astype(BF16) for s in range(6)], axis=1)
    lane = iota((DOM, LANES), 1)
    source = iota((DOM, DOM), 1).astype(F32)
    place = (iota((DOM, 256), 1) // CASES).astype(F32)
    chosen, keep = [], []
    for i in range(P_SIZE):
        device = jnp.sum(jnp.where(lane == 64 + i, info, 0.0), axis=1, keepdims=True)
        row = jnp.sum(jnp.where(lane == 76 + i, info, 0.0), axis=1, keepdims=True)
        chosen.append(one_hot(device == source))
        keep.append(row == place)
    taken = dot(jnp.concatenate(chosen, axis=0), rows)
    fold = one_hot(iota((256, LANES), 0) % CASES == iota((256, LANES), 1) % CASES)
    for k in range(3):
        kept = jnp.concatenate(
            [jnp.where(keep[i], taken[i * DOM:(i + 1) * DOM, k * 256:(k + 1) * 256], 0.0).astype(BF16)
             for i in range(P_SIZE)], axis=0)
        copies = dot(kept, fold)
        for t, count in ((0, LEAF), (1, ANC)):
            moved = jnp.zeros((DOM, LANES), F32)
            for i in range(count):
                at = (LEAF * t + i) * DOM
                moved = jnp.where(lane // CASES == i, copies[at:at + DOM], moved)
            message[pl.ds(2 * k + t, DOM, stride=ROWS), :] = moved
    for s in (6, 7):
        message[pl.ds(s, DOM, stride=ROWS), :] = jnp.zeros((DOM, LANES), F32)
    out[...] = message[...].astype(BF16)


def fetch_kernel(notes, tiles, out, sems):
    step = PAIRS * LEAF // 8
    copies = [pltpu.make_async_copy(tiles.at[pl.ds(n * step, step)], out.at[pl.ds(n * step, step)], sems.at[n])
              for n in range(LEAF // 2)]
    for copy in copies:
        copy.start()
    for copy in copies:
        copy.wait()


def update_kernel(received, inverses, tiles, early, level, ancestors, out,
                  wide, leaf, rest, right, near, sems, partial):
    copies = [pltpu.make_async_copy(tiles.at[pl.ds(k * PAIRS, PAIRS)], near.at[pl.ds((k - LEAF // 2) * PAIRS, PAIRS)],
                                    sems.at[k - LEAF // 2]) for k in range(LEAF // 2, LEAF)]
    for copy in copies:
        copy.start()
    wide[...] = received[...].astype(F32)
    for k in range(3):
        for par in range(2):
            at = pl.ds(2 * k + par, 32, stride=6)
            leaf[at, :] = wide[pl.ds(par * 256 + 2 * k, 32, stride=ROWS), :]
            rest[at, :] = wide[pl.ds(par * 256 + 2 * k + 1, 32, stride=ROWS), :]

    def doubled(x):
        zeros = jnp.zeros_like(x)
        return jnp.concatenate(
            [jnp.concatenate([x, zeros], axis=1), jnp.concatenate([zeros, x], axis=1)], axis=0)

    def left(ref, start, count):
        return jnp.concatenate(
            [ref[pl.ds(start, count), t].reshape(count * 8, LANES) for t in range(3)], axis=1)

    solved = dot(left(inverses, 0, PAIRS), doubled(leaf[...].astype(BF16)))
    own = iota((768, 256), 0) % 8 == (iota((768, 256), 1) % LANES) // 16
    solved = jnp.where(own, solved, 0.0).astype(BF16)
    gather = one_hot(iota((B, 768), 1) // 8 == iota((B, 768), 0) // 2)
    solved = dot(gather, solved)
    solved = jnp.where(iota((B, LANES), 0) % 2 == 0, solved[:, :LANES], solved[:, LANES:])
    unit = one_hot(iota((LANES, LANES), 0) == iota((LANES, LANES), 1))
    level[...] = lax.dot_general(unit, solved.astype(BF16), NT, preferred_element_type=F32).astype(BF16)
    ancestors[...] = lax.dot_general(
        unit[:64], rest[...].astype(BF16), NT, preferred_element_type=F32)
    owner = iota((B, LANES), 1) // 16
    for k in range(LEAF):
        right[k * 384:(k + 1) * 384] = doubled(jnp.where(owner == k, solved, 0.0)).astype(BF16)
    step, band = LEAF // 2, PAIRS // 2
    for first in range(0, LEAF, step):
        if first:
            for copy in copies:
                copy.wait()
        for r in range(0, PAIRS, band):
            at = slice(r * 8, (r + band) * 8)
            wide_left = jnp.concatenate(
                [left(near if first else early, k * PAIRS + r, band) for k in range(step)], axis=1)
            total = dot(wide_left, right[first * 384:(first + step) * 384])
            if first == 0:
                partial[at] = total
            else:
                out[at] = (partial[at] + total).astype(BF16)


def sum_kernel(received, targets, squares, out, squares_out, right):
    squares_out[...] = squares[...]
    select = one_hot(targets[...] == iota((256, 512), 0).astype(F32))
    group = iota((64, LANES), 1) // CASES
    for tile in range(3):
        parts = []
        for pair in range(tile * 4, tile * 4 + 4):
            rows = jnp.concatenate(
                [received[s, pair * 8:(pair + 1) * 8, :].astype(F32) for s in range(GROUP)], axis=0)
            parts.extend([rows[:, :LANES], rows[:, LANES:]])
        for step in (4, 2, 1):
            upper = (group // step) % 2 == 1
            turned = list(parts)
            for i in range(8):
                if not i & step:
                    a, b = parts[i], parts[i + step]
                    turned[i] = jnp.where(upper, pltpu.roll(b, step * CASES, 1), a)
                    turned[i + step] = jnp.where(upper, b, pltpu.roll(a, LANES - step * CASES, 1))
            parts = turned
        for k in range(LEAF):
            right[k * 64:(k + 1) * 64, tile * LANES:(tile + 1) * LANES] = parts[k].astype(BF16)
    out[...] = dot(select, right[...]).reshape(DOM, ANC, 384).astype(BF16)


def final_kernel(received, ancestors, out):
    place = iota((32, 256), 1)
    source, block = place // ANC, place % ANC
    group = source // (N_Z * N_CORE) * N_CORE + source % N_CORE
    row = iota((32, 256), 0)
    pick = one_hot((row % ANC == block) & (row // ANC == group))
    summed = dot(pick, received[...])
    count = ANC * CASES
    own = iota((count, 384), 1) % CASES == iota((count, 384), 0) % CASES
    sides = ([], [])
    for q in range(GROUP):
        left = jnp.concatenate(
            [jnp.broadcast_to(summed[q * ANC + t:q * ANC + t + 1], (CASES, 384)) for t in range(ANC)], axis=0)
        for side, part in zip(sides, halves(jnp.where(own, left, 0.0))):
            side.append(part)
    column = one_hot(iota((384, 24), 1) == iota((384, 24), 0) // CASES)
    both = dot(jnp.concatenate(sides[0] + sides[1], axis=0), column)
    both = both[:GROUP * count] + both[GROUP * count:]
    out[...] = ancestors[...] - jnp.concatenate(
        [both[q * count:(q + 1) * count] for q in range(GROUP)], axis=1)


def call(kernel, name, shapes, in_specs, scratch, megabytes=16, cost=None):
    outs = [jax.ShapeDtypeStruct(*s) for s in shapes]
    return pl.pallas_call(
        kernel,
        out_shape=outs,
        in_specs=in_specs,
        out_specs=[pl.BlockSpec(memory_space=pltpu.VMEM)] * len(outs),
        scratch_shapes=scratch,
        compiler_params=pltpu.CompilerParams(vmem_limit_bytes=megabytes * 2**20),
        cost_estimate=cost,
        name=name,
    )


def on_device(solution, loads, blocks, columns, row_source, inverses, tiles, targets):
    vmem = pl.BlockSpec(memory_space=pltpu.VMEM)
    smem = pl.BlockSpec(memory_space=pltpu.SMEM)
    hbm = pl.BlockSpec(memory_space=pltpu.HBM)
    dma = pltpu.SemaphoreType.DMA
    device = lax.axis_index("dom")
    far = lax.ppermute(solution, "dom", [(i, i + 1 if i % 2 else i - 1) for i in range(1, DOM - 1)])
    chip = lax.ppermute(solution, "dom", [(i, i ^ 1) for i in range(DOM)])
    local = columns.T - (device * P_SIZE - P_SIZE)
    turn = jnp.where(local < P_SIZE, 2 * P_SIZE, jnp.where(local < 2 * P_SIZE, 0, -2 * P_SIZE))
    local = local + jnp.where(device % 2 == 0, turn, 0)
    table = jnp.concatenate([
        jnp.pad(local, ((0, 0), (0, LANES - P_SIZE))),
        jnp.pad(row_source.reshape(1, P_SIZE), ((0, 3), (0, LANES - P_SIZE))),
        jnp.pad(targets, ((0, 0), (0, LANES - UPD)))], axis=0)
    natural = blocks.reshape(P_SIZE, NNZ, 288, LANES).transpose(0, 2, 1, 3).reshape(P_SIZE * 1152, LANES)
    natural_inverses = inverses.reshape(LEAF, 288, LANES).transpose(1, 0, 2).reshape(PAIRS, 3, LEAF, LANES)
    natural_tiles = tiles.reshape(LEAF, UPD, 288, LANES).transpose(0, 2, 1, 3)
    natural_tiles = natural_tiles.reshape(LEAF * PAIRS, 3, UPD, LANES)
    (lanes,) = call(
        lane_kernel, "lanes", [((ROWS, LANES), jnp.int32)], [], [], 16,
        pl.CostEstimate(flops=3 * 10**10, bytes_accessed=10**6, transcendentals=0))()
    high, low, cells, start, info = call(
        split_kernel, "split",
        [((P_SIZE, PAIRS, 1536), BF16), ((P_SIZE, PAIRS, 1536), BF16), ((2 * P_SIZE, 64, 384), BF16),
         ((P_SIZE, PAIRS, 64), F32), ((1, LANES), F32)],
        [smem, hbm] + [vmem] * 4,
        [pltpu.VMEM((P_SIZE, 64, 384), BF16), pltpu.VMEM((P_SIZE * 1152, LANES), F32), dma((P_SIZE,))], 41,
        pl.CostEstimate(flops=10**9, bytes_accessed=14 * 10**6, transcendentals=0),
    )(table, natural, chip, solution, loads, lanes)
    (message,) = call(
        residual_kernel, "residual", [((DOM * ROWS, LANES), BF16)],
        [smem] + [vmem] * 6,
        [pltpu.VMEM((3 * P_SIZE, 64, 384), BF16), pltpu.VMEM((DOM * ROWS, LANES), F32)], 16,
    )(table, high, low, cells, start, info, far)

    def exchange(x):
        x = x.reshape(DOM, ROWS, LANES)
        return lax.all_to_all(x, "dom", 0, 0, tiled=True).reshape(DOM * ROWS, LANES)

    def across(x, step):
        return x + lax.ppermute(x, "rhs", [(i, i ^ step) for i in range(4)])

    message, notes, squares = call(
        permute_kernel, "permute",
        [((DOM * ROWS, LANES), BF16), ((DOM, LANES), F32), ((1, LANES), F32)], [vmem],
        [pltpu.VMEM((DOM * ROWS, LANES), F32), pltpu.VMEM((DOM * ROWS, LANES), F32)], 16,
        pl.CostEstimate(flops=4 * 10**9, bytes_accessed=10**6, transcendentals=0),
    )(exchange(message))

    half = (LEAF // 2 * PAIRS, 3, UPD, LANES)
    (early,) = call(fetch_kernel, "fetch", [(half, BF16)], [vmem, hbm], [dma((LEAF // 2,))], 50,
                    pl.CostEstimate(flops=2 * 10**9, bytes_accessed=10**6, transcendentals=0),
                    )(notes, natural_tiles)
    level, ancestors, message = call(
        update_kernel, "update",
        [((LEAF * CASES, B), BF16), ((ANC * CASES, B), F32), ((PAIRS * UPD, 256), BF16)],
        [vmem, vmem, hbm, vmem],
        [pltpu.VMEM((DOM * ROWS, LANES), F32), pltpu.VMEM((B, LANES), F32), pltpu.VMEM((B, LANES), F32),
         pltpu.VMEM((LEAF * 384, 256), BF16), pltpu.VMEM(half, BF16),
         dma((LEAF // 2,)), pltpu.VMEM((PAIRS * UPD, 256), F32)], 48,
    )(exchange(message), natural_inverses, natural_tiles, early)

    groups = [[(x * N_Z + z) * N_CORE + c for x in range(N_X) for c in range(N_CORE)] for z in range(N_Z)]
    received = lax.all_to_all(
        message.reshape(GROUP, 96, 256), "dom", 0, 0, axis_index_groups=groups, tiled=True)
    z = (device // N_CORE) % N_Z
    near = lax.dynamic_index_in_dim(notes.reshape(N_X, N_Z, N_CORE, LANES), z, axis=1, keepdims=False)
    near = near.reshape(GROUP, LANES)[:, :LEAF * UPD].reshape(GROUP, LEAF, UPD)
    near = near.transpose(1, 0, 2).reshape(1, LEAF * GROUP * UPD)
    sums, squares = call(
        sum_kernel, "sum", [((DOM, ANC, 384), BF16), ((1, LANES), F32)], [vmem] * 3,
        [pltpu.VMEM((512, 384), BF16)],
    )(received, near, across(squares, 1))
    residual_rms = jnp.sqrt(across(squares, 2)[0, 0] / (DOM * P_SIZE * CASES * 4 * B))
    sums = lax.all_to_all(sums, "dom", 0, 0, tiled=True)
    (ancestor_rhs,) = call(final_kernel, "final", [((ANC * CASES, B), F32)], [vmem] * 2, [])(
        sums.reshape(DOM * ANC, 384), ancestors)
    return (level.reshape(LEAF, CASES, B), ancestor_rhs.reshape(ANC, CASES, B), residual_rms)


def solution(mesh):
    placed = (
        P("dom", "rhs", None),
        P("dom", "rhs", None),
        P("dom", None, None),
        P("dom", None),
        P("dom"),
        P("dom", None),
        P("dom", None, None),
        P("dom", None),
    )
    return jax.shard_map(
        on_device,
        mesh=mesh,
        in_specs=placed,
        out_specs=(P("dom", "rhs", None), P("dom", "rhs", None), P()),
        check_vma=False,
    )
```

```python
import jax
import jax.numpy as jnp
from jax import lax
from jax.experimental import pallas as pl
from jax.experimental.pallas import tpu as pltpu
from jax.sharding import PartitionSpec as P

B = 192
LEAF = 8
ANC = 4
NNZ = 4
UPD = 8
P_SIZE = 12
CASES = 16
DOM = 64
N_X, N_Z, N_CORE = 4, 8, 2
GROUP = N_X * N_CORE
LANES = 128
ROWS = 8
PAIRS = B // 2
BF16 = jnp.bfloat16
F32 = jnp.float32
NT = (((1,), (1,)), ((), ()))


def iota(shape, dim):
    return lax.broadcasted_iota(jnp.int32, shape, dim)


def one_hot(condition):
    return jnp.where(condition, 1.0, 0.0).astype(BF16)


def halves(x):
    high = x.astype(BF16)
    return high, (x - high.astype(F32)).astype(BF16)


def dot(a, b):
    return jnp.dot(a, b, preferred_element_type=F32)


def put_cells(x, cells, slot):
    wide, narrow = x[:, :LANES], jnp.concatenate([x[:, LANES:], jnp.zeros((CASES, 64), F32)], axis=1)
    lower = iota((CASES, LANES), 1) < 64
    zeros = jnp.zeros((CASES, LANES), F32)
    turned = pltpu.roll(wide, 64, 1)
    lines = (
        (wide, narrow, zeros),
        (zeros, jnp.where(lower, 0.0, turned), jnp.where(lower, turned, pltpu.roll(narrow, 64, 1))),
    )
    for par in range(2):
        for t in range(3):
            for part, value in enumerate(halves(lines[par][t])):
                row = (2 * par + part) * CASES
                cells[slot, row:row + CASES, t * LANES:(t + 1) * LANES] = value


def lane_kernel(out):
    out[...] = iota((ROWS, LANES), 1)


def split_kernel(table, blocks, chip, own, loads, lanes, high, low, cells, start, info,
                 load_cells, wide, sems):
    count = NNZ * 288
    copies = [pltpu.make_async_copy(blocks.at[pl.ds(g * count, count)], wide.at[pl.ds(g * count, count)],
                                    sems.at[g]) for g in range(P_SIZE)]
    for copy in copies:
        copy.start()
    for i in range(P_SIZE):
        put_cells(loads[i], load_cells, i)
        put_cells(chip[i], cells, i)
        put_cells(own[i], cells, P_SIZE + i)
    unit_row, unit_col = iota((PAIRS, 384), 0), iota((PAIRS, 384), 1)
    pair = (unit_row % 32) * 3 + unit_row // 32
    unit = one_hot((unit_col == 2 * pair) | (unit_col == 2 * pair + B + 1))
    for g in range(P_SIZE):
        start[g] = lax.dot_general(unit, load_cells[g], NT, preferred_element_type=F32)
    lane = lanes[...]
    notes = jnp.zeros((ROWS, LANES), jnp.int32)
    for k in range(LEAF):
        for m in range(UPD):
            notes = jnp.where(lane == k * UPD + m, table[8 + k, m], notes)
    for i in range(P_SIZE):
        source = table[4, i]
        notes = jnp.where(lane == 64 + i, source // P_SIZE, notes)
        notes = jnp.where(lane == 76 + i, source % P_SIZE, notes)
    info[...] = notes.astype(F32)[:1]

    for g in range(P_SIZE):
        if g % 2 == 0:
            for copy in copies[g:g + 2]:
                copy.wait()
        for j in range(NNZ):
            for t in range(3):
                tall = jnp.concatenate(
                    [wide[pl.ds(g * count + 12 * k + j + 4 * t, 32, stride=36), :] for k in range(3)], axis=0)
                at = (g, slice(None), slice(j * 384 + t * LANES, j * 384 + (t + 1) * LANES))
                high[at], low[at] = halves(tall)


def residual_kernel(table, high, low, near, start, info, far, out, cells, message):
    for i in range(P_SIZE):
        cells[i] = near[i]
        cells[P_SIZE + i] = near[P_SIZE + i]
        put_cells(far[i], cells, 2 * P_SIZE + i)

    residuals = ([], [])
    for g in range(P_SIZE):
        right = jnp.concatenate([cells[table[j, g]] for j in range(NNZ)], axis=1)
        total = start[g]
        for side in (high, low):
            total = total - lax.dot_general(side[g], right, NT, preferred_element_type=F32)
        for par in range(2):
            one = total[:, par * 32:par * 32 + 16] + total[:, par * 32 + 16:par * 32 + 32]
            residuals[par].append(one)

    squares = jnp.zeros((PAIRS, LANES), F32)
    for par in range(2):
        ones = residuals[par] + [jnp.zeros((PAIRS, CASES), F32)] * 4
        for t in range(2):
            tile = jnp.concatenate(ones[8 * t:8 * t + 8], axis=1)
            squares = squares + tile * tile
            for k in range(3):
                message[k, pl.ds(par * 64 + t, 32, stride=2), :] = tile[k * 32:(k + 1) * 32]
    whole = jnp.sum(squares).reshape(1, 1)
    first = whole.astype(BF16).astype(F32)
    second = (whole - first).astype(BF16).astype(F32)
    third = whole - first - second
    lane = iota((DOM, LANES), 1)
    notes = jnp.broadcast_to(info[...], (DOM, LANES))
    parts = jnp.where(lane == 64, first, jnp.where(lane == 65, second, jnp.where(lane == 66, third, 0.0)))
    for k, extra in enumerate((pltpu.roll(notes, 64, 1), notes, parts)):
        at = pl.ds(1, DOM, stride=2)
        message[k, at, :] = jnp.where(lane < 64, message[k, at, :], extra)
    out[...] = packed(message)


def packed(message):
    whole = jnp.concatenate([message[k] for k in range(3)], axis=1)
    return whole.reshape(DOM, 2, 384).astype(BF16)


def unpacked(received, wide):
    whole = received[...].astype(F32).reshape(2 * DOM, 384)
    for k in range(3):
        wide[k] = whole[:, k * LANES:(k + 1) * LANES]


def permute_kernel(received, out, notes, squares, wide, message):
    unpacked(received, wide)
    odd = pl.ds(1, DOM, stride=2)
    info = wide[1, odd, :]
    notes[...] = pltpu.roll(wide[0, odd, :], 64, 1)
    upper = iota((DOM, LANES), 1) >= 64
    squares[...] = jnp.broadcast_to(
        jnp.sum(jnp.where(upper, wide[2, odd, :], 0.0)).reshape(1, 1), (1, LANES))
    rows = jnp.concatenate(
        [wide[k, pl.ds(t, DOM, stride=2), :].astype(BF16) for k in range(3) for t in range(2)], axis=1)
    lane = iota((DOM, LANES), 1)
    source = iota((DOM, DOM), 1).astype(F32)
    place = (iota((DOM, 256), 1) // CASES).astype(F32)
    chosen, keep = [], []
    for i in range(P_SIZE):
        device = jnp.sum(jnp.where(lane == 64 + i, info, 0.0), axis=1, keepdims=True)
        row = jnp.sum(jnp.where(lane == 76 + i, info, 0.0), axis=1, keepdims=True)
        chosen.append(one_hot(device == source))
        keep.append(row == place)
    taken = dot(jnp.concatenate(chosen, axis=0), rows)
    fold = one_hot(iota((256, LANES), 0) % CASES == iota((256, LANES), 1) % CASES)
    for k in range(3):
        kept = jnp.concatenate(
            [jnp.where(keep[i], taken[i * DOM:(i + 1) * DOM, k * 256:(k + 1) * 256], 0.0).astype(BF16)
             for i in range(P_SIZE)], axis=0)
        copies = dot(kept, fold)
        for t, count in ((0, LEAF), (1, ANC)):
            moved = jnp.zeros((DOM, LANES), F32)
            for i in range(count):
                at = (LEAF * t + i) * DOM
                moved = jnp.where(lane // CASES == i, copies[at:at + DOM], moved)
            message[k, pl.ds(t, DOM, stride=2), :] = moved
    out[...] = packed(message)


def fetch_kernel(notes, tiles, out, sems):
    step = PAIRS * LEAF // 8
    copies = [pltpu.make_async_copy(tiles.at[pl.ds(n * step, step)], out.at[pl.ds(n * step, step)], sems.at[n])
              for n in range(LEAF // 2)]
    for copy in copies:
        copy.start()
    for copy in copies:
        copy.wait()


def update_kernel(received, inverses, tiles, early, level, ancestors, out,
                  wide, leaf, rest, right, near, sems, partial):
    copies = [pltpu.make_async_copy(tiles.at[pl.ds(k * PAIRS, PAIRS)], near.at[pl.ds((k - LEAF // 2) * PAIRS, PAIRS)],
                                    sems.at[k - LEAF // 2]) for k in range(LEAF // 2, LEAF)]
    for copy in copies:
        copy.start()
    unpacked(received, wide)
    for k in range(3):
        for par in range(2):
            at = pl.ds(2 * k + par, 32, stride=6)
            leaf[at, :] = wide[k, pl.ds(par * 64, 32, stride=2), :]
            rest[at, :] = wide[k, pl.ds(par * 64 + 1, 32, stride=2), :]

    def doubled(x):
        zeros = jnp.zeros_like(x)
        return jnp.concatenate(
            [jnp.concatenate([x, zeros], axis=1), jnp.concatenate([zeros, x], axis=1)], axis=0)

    def left(ref, start, count):
        return jnp.concatenate(
            [ref[pl.ds(start, count), t].reshape(count * 8, LANES) for t in range(3)], axis=1)

    solved = dot(left(inverses, 0, PAIRS), doubled(leaf[...].astype(BF16)))
    own = iota((768, 256), 0) % 8 == (iota((768, 256), 1) % LANES) // 16
    solved = jnp.where(own, solved, 0.0).astype(BF16)
    gather = one_hot(iota((B, 768), 1) // 8 == iota((B, 768), 0) // 2)
    solved = dot(gather, solved)
    solved = jnp.where(iota((B, LANES), 0) % 2 == 0, solved[:, :LANES], solved[:, LANES:])
    unit = one_hot(iota((LANES, LANES), 0) == iota((LANES, LANES), 1))
    level[...] = lax.dot_general(unit, solved.astype(BF16), NT, preferred_element_type=F32).astype(BF16)
    ancestors[...] = lax.dot_general(
        unit[:64], rest[...].astype(BF16), NT, preferred_element_type=F32)
    owner = iota((B, LANES), 1) // 16
    for k in range(LEAF):
        right[k * 384:(k + 1) * 384] = doubled(jnp.where(owner == k, solved, 0.0)).astype(BF16)
    step, band = LEAF // 2, PAIRS // 2
    for first in range(0, LEAF, step):
        if first:
            for copy in copies:
                copy.wait()
        for r in range(0, PAIRS, band):
            at = slice(r * 8, (r + band) * 8)
            wide_left = jnp.concatenate(
                [left(near if first else early, k * PAIRS + r, band) for k in range(step)], axis=1)
            total = dot(wide_left, right[first * 384:(first + step) * 384])
            if first == 0:
                partial[at] = total
            else:
                out[at] = (partial[at] + total).astype(BF16)


def sum_kernel(received, targets, squares, out, squares_out, right):
    squares_out[...] = squares[...]
    select = one_hot(targets[...] == iota((256, 512), 0).astype(F32))
    group = iota((64, LANES), 1) // CASES
    for tile in range(3):
        parts = []
        for pair in range(tile * 4, tile * 4 + 4):
            rows = jnp.concatenate(
                [received[s, pair * 8:(pair + 1) * 8, :].astype(F32) for s in range(GROUP)], axis=0)
            parts.extend([rows[:, :LANES], rows[:, LANES:]])
        for step in (4, 2, 1):
            upper = (group // step) % 2 == 1
            turned = list(parts)
            for i in range(8):
                if not i & step:
                    a, b = parts[i], parts[i + step]
                    turned[i] = jnp.where(upper, pltpu.roll(b, step * CASES, 1), a)
                    turned[i + step] = jnp.where(upper, b, pltpu.roll(a, LANES - step * CASES, 1))
            parts = turned
        for k in range(LEAF):
            right[k * 64:(k + 1) * 64, tile * LANES:(tile + 1) * LANES] = parts[k].astype(BF16)
    out[...] = dot(select, right[...]).reshape(DOM, ANC, 384).astype(BF16)


def final_kernel(received, ancestors, out):
    place = iota((32, 256), 1)
    source, block = place // ANC, place % ANC
    group = source // (N_Z * N_CORE) * N_CORE + source % N_CORE
    row = iota((32, 256), 0)
    pick = one_hot((row % ANC == block) & (row // ANC == group))
    summed = dot(pick, received[...])
    count = ANC * CASES
    own = iota((count, 384), 1) % CASES == iota((count, 384), 0) % CASES
    sides = ([], [])
    for q in range(GROUP):
        left = jnp.concatenate(
            [jnp.broadcast_to(summed[q * ANC + t:q * ANC + t + 1], (CASES, 384)) for t in range(ANC)], axis=0)
        for side, part in zip(sides, halves(jnp.where(own, left, 0.0))):
            side.append(part)
    column = one_hot(iota((384, 24), 1) == iota((384, 24), 0) // CASES)
    both = dot(jnp.concatenate(sides[0] + sides[1], axis=0), column)
    both = both[:GROUP * count] + both[GROUP * count:]
    out[...] = ancestors[...] - jnp.concatenate(
        [both[q * count:(q + 1) * count] for q in range(GROUP)], axis=1)


def call(kernel, name, shapes, in_specs, scratch, megabytes=16, cost=None):
    outs = [jax.ShapeDtypeStruct(*s) for s in shapes]
    return pl.pallas_call(
        kernel,
        out_shape=outs,
        in_specs=in_specs,
        out_specs=[pl.BlockSpec(memory_space=pltpu.VMEM)] * len(outs),
        scratch_shapes=scratch,
        compiler_params=pltpu.CompilerParams(vmem_limit_bytes=megabytes * 2**20),
        cost_estimate=cost,
        name=name,
    )


def on_device(solution, loads, blocks, columns, row_source, inverses, tiles, targets):
    vmem = pl.BlockSpec(memory_space=pltpu.VMEM)
    smem = pl.BlockSpec(memory_space=pltpu.SMEM)
    hbm = pl.BlockSpec(memory_space=pltpu.HBM)
    dma = pltpu.SemaphoreType.DMA
    device = lax.axis_index("dom")
    far = lax.ppermute(solution, "dom", [(i, i + 1 if i % 2 else i - 1) for i in range(1, DOM - 1)])
    chip = lax.ppermute(solution, "dom", [(i, i ^ 1) for i in range(DOM)])
    local = columns.T - (device * P_SIZE - P_SIZE)
    turn = jnp.where(local < P_SIZE, 2 * P_SIZE, jnp.where(local < 2 * P_SIZE, 0, -2 * P_SIZE))
    local = local + jnp.where(device % 2 == 0, turn, 0)
    table = jnp.concatenate([
        jnp.pad(local, ((0, 0), (0, LANES - P_SIZE))),
        jnp.pad(row_source.reshape(1, P_SIZE), ((0, 3), (0, LANES - P_SIZE))),
        jnp.pad(targets, ((0, 0), (0, LANES - UPD)))], axis=0)
    natural = blocks.reshape(P_SIZE, NNZ, 288, LANES).transpose(0, 2, 1, 3).reshape(P_SIZE * 1152, LANES)
    natural_inverses = inverses.reshape(LEAF, 288, LANES).transpose(1, 0, 2).reshape(PAIRS, 3, LEAF, LANES)
    natural_tiles = tiles.reshape(LEAF, UPD, 288, LANES).transpose(0, 2, 1, 3)
    natural_tiles = natural_tiles.reshape(LEAF * PAIRS, 3, UPD, LANES)
    (lanes,) = call(
        lane_kernel, "lanes", [((ROWS, LANES), jnp.int32)], [], [], 16,
        pl.CostEstimate(flops=3 * 10**10, bytes_accessed=10**6, transcendentals=0))()
    high, low, cells, start, info = call(
        split_kernel, "split",
        [((P_SIZE, PAIRS, 1536), BF16), ((P_SIZE, PAIRS, 1536), BF16), ((2 * P_SIZE, 64, 384), BF16),
         ((P_SIZE, PAIRS, 64), F32), ((1, LANES), F32)],
        [smem, hbm] + [vmem] * 4,
        [pltpu.VMEM((P_SIZE, 64, 384), BF16), pltpu.VMEM((P_SIZE * 1152, LANES), F32), dma((P_SIZE,))], 41,
        pl.CostEstimate(flops=10**9, bytes_accessed=14 * 10**6, transcendentals=0),
    )(table, natural, chip, solution, loads, lanes)
    (message,) = call(
        residual_kernel, "residual", [((DOM, 2, 384), BF16)],
        [smem] + [vmem] * 6,
        [pltpu.VMEM((3 * P_SIZE, 64, 384), BF16), pltpu.VMEM((3, 2 * DOM, LANES), F32)], 16,
    )(table, high, low, cells, start, info, far)

    def exchange(x):
        return lax.all_to_all(x, "dom", 0, 0, tiled=True)

    def across(x, step):
        return x + lax.ppermute(x, "rhs", [(i, i ^ step) for i in range(4)])

    message, notes, squares = call(
        permute_kernel, "permute",
        [((DOM, 2, 384), BF16), ((DOM, LANES), F32), ((1, LANES), F32)], [vmem],
        [pltpu.VMEM((3, 2 * DOM, LANES), F32), pltpu.VMEM((3, 2 * DOM, LANES), F32)], 16,
        pl.CostEstimate(flops=4 * 10**9, bytes_accessed=10**6, transcendentals=0),
    )(exchange(message))

    half = (LEAF // 2 * PAIRS, 3, UPD, LANES)
    (early,) = call(fetch_kernel, "fetch", [(half, BF16)], [vmem, hbm], [dma((LEAF // 2,))], 50,
                    pl.CostEstimate(flops=2 * 10**9, bytes_accessed=10**6, transcendentals=0),
                    )(notes, natural_tiles)
    level, ancestors, message = call(
        update_kernel, "update",
        [((LEAF * CASES, B), BF16), ((ANC * CASES, B), F32), ((PAIRS * UPD, 256), BF16)],
        [vmem, vmem, hbm, vmem],
        [pltpu.VMEM((3, 2 * DOM, LANES), F32), pltpu.VMEM((B, LANES), F32), pltpu.VMEM((B, LANES), F32),
         pltpu.VMEM((LEAF * 384, 256), BF16), pltpu.VMEM(half, BF16),
         dma((LEAF // 2,)), pltpu.VMEM((PAIRS * UPD, 256), F32)], 48,
    )(exchange(message), natural_inverses, natural_tiles, early)

    groups = [[(x * N_Z + z) * N_CORE + c for x in range(N_X) for c in range(N_CORE)] for z in range(N_Z)]
    received = lax.all_to_all(
        message.reshape(GROUP, 96, 256), "dom", 0, 0, axis_index_groups=groups, tiled=True)
    z = (device // N_CORE) % N_Z
    near = lax.dynamic_index_in_dim(notes.reshape(N_X, N_Z, N_CORE, LANES), z, axis=1, keepdims=False)
    near = near.reshape(GROUP, LANES)[:, :LEAF * UPD].reshape(GROUP, LEAF, UPD)
    near = near.transpose(1, 0, 2).reshape(1, LEAF * GROUP * UPD)
    sums, squares = call(
        sum_kernel, "sum", [((DOM, ANC, 384), BF16), ((1, LANES), F32)], [vmem] * 3,
        [pltpu.VMEM((512, 384), BF16)],
    )(received, near, across(squares, 1))
    residual_rms = jnp.sqrt(across(squares, 2)[0, 0] / (DOM * P_SIZE * CASES * 4 * B))
    sums = lax.all_to_all(sums, "dom", 0, 0, tiled=True)
    (ancestor_rhs,) = call(final_kernel, "final", [((ANC * CASES, B), F32)], [vmem] * 2, [])(
        sums.reshape(DOM * ANC, 384), ancestors)
    return (level.reshape(LEAF, CASES, B), ancestor_rhs.reshape(ANC, CASES, B), residual_rms)


def solution(mesh):
    placed = (
        P("dom", "rhs", None),
        P("dom", "rhs", None),
        P("dom", None, None),
        P("dom", None),
        P("dom"),
        P("dom", None),
        P("dom", None, None),
        P("dom", None),
    )
    return jax.shard_map(
        on_device,
        mesh=mesh,
        in_specs=placed,
        out_specs=(P("dom", "rhs", None), P("dom", "rhs", None), P()),
        check_vma=False,
    )
```

```python
import jax
import jax.numpy as jnp
from jax import lax
from jax.experimental import pallas as pl
from jax.experimental.pallas import tpu as pltpu
from jax.sharding import PartitionSpec as P

B = 192
LEAF = 8
ANC = 4
NNZ = 4
UPD = 8
P_SIZE = 12
CASES = 16
DOM = 64
N_X, N_Z, N_CORE = 4, 8, 2
GROUP = N_X * N_CORE
LANES = 128
ROWS = 8
PAIRS = B // 2
BF16 = jnp.bfloat16
F32 = jnp.float32
NT = (((1,), (1,)), ((), ()))


def iota(shape, dim):
    return lax.broadcasted_iota(jnp.int32, shape, dim)


def one_hot(condition):
    return jnp.where(condition, 1.0, 0.0).astype(BF16)


def halves(x):
    high = x.astype(BF16)
    return high, (x - high.astype(F32)).astype(BF16)


def dot(a, b):
    return jnp.dot(a, b, preferred_element_type=F32)


def put_cells(x, cells, slot):
    wide, narrow = x[:, :LANES], jnp.concatenate([x[:, LANES:], jnp.zeros((CASES, 64), F32)], axis=1)
    lower = iota((CASES, LANES), 1) < 64
    zeros = jnp.zeros((CASES, LANES), F32)
    turned = pltpu.roll(wide, 64, 1)
    lines = (
        (wide, narrow, zeros),
        (zeros, jnp.where(lower, 0.0, turned), jnp.where(lower, turned, pltpu.roll(narrow, 64, 1))),
    )
    for par in range(2):
        for t in range(3):
            for part, value in enumerate(halves(lines[par][t])):
                row = (2 * par + part) * CASES
                cells[slot, row:row + CASES, t * LANES:(t + 1) * LANES] = value


def lane_kernel(out):
    out[...] = iota((ROWS, LANES), 1)


def split_kernel(table, blocks, chip, own, loads, lanes, high, low, cells, start, info,
                 load_cells, wide, sems):
    count = NNZ * 288
    copies = [pltpu.make_async_copy(blocks.at[pl.ds(g * count, count)], wide.at[pl.ds(g * count, count)],
                                    sems.at[g]) for g in range(P_SIZE)]
    for copy in copies:
        copy.start()
    for i in range(P_SIZE):
        put_cells(loads[i], load_cells, i)
        put_cells(chip[i], cells, i)
        put_cells(own[i], cells, P_SIZE + i)
    unit_row, unit_col = iota((PAIRS, 384), 0), iota((PAIRS, 384), 1)
    pair = (unit_row % 32) * 3 + unit_row // 32
    unit = one_hot((unit_col == 2 * pair) | (unit_col == 2 * pair + B + 1))
    for g in range(P_SIZE):
        start[g] = lax.dot_general(unit, load_cells[g], NT, preferred_element_type=F32)
    lane = lanes[...]
    notes = jnp.zeros((ROWS, LANES), jnp.int32)
    for k in range(LEAF):
        for m in range(UPD):
            notes = jnp.where(lane == k * UPD + m, table[8 + k, m], notes)
    for i in range(P_SIZE):
        source = table[4, i]
        notes = jnp.where(lane == 64 + i, source // P_SIZE, notes)
        notes = jnp.where(lane == 76 + i, source % P_SIZE, notes)
    info[...] = notes.astype(F32)[:1]

    for g in range(P_SIZE):
        if g % 2 == 0:
            for copy in copies[g:g + 2]:
                copy.wait()
        for j in range(NNZ):
            for t in range(3):
                tall = jnp.concatenate(
                    [wide[pl.ds(g * count + 12 * k + j + 4 * t, 32, stride=36), :] for k in range(3)], axis=0)
                at = (g, slice(None), slice(j * 384 + t * LANES, j * 384 + (t + 1) * LANES))
                high[at], low[at] = halves(tall)


def residual_kernel(table, high, low, near, start, info, far, out, cells, message):
    for i in range(P_SIZE):
        cells[i] = near[i]
        cells[P_SIZE + i] = near[P_SIZE + i]
        put_cells(far[i], cells, 2 * P_SIZE + i)

    residuals = ([], [])
    for g in range(P_SIZE):
        right = jnp.concatenate([cells[table[j, g]] for j in range(NNZ)], axis=1)
        total = start[g]
        for side in (high, low):
            total = total - lax.dot_general(side[g], right, NT, preferred_element_type=F32)
        for par in range(2):
            one = total[:, par * 32:par * 32 + 16] + total[:, par * 32 + 16:par * 32 + 32]
            residuals[par].append(one)

    squares = jnp.zeros((PAIRS, LANES), F32)
    for par in range(2):
        ones = residuals[par] + [jnp.zeros((PAIRS, CASES), F32)] * 4
        for t in range(2):
            tile = jnp.concatenate(ones[8 * t:8 * t + 8], axis=1)
            squares = squares + tile * tile
            for k in range(3):
                message[k, pl.ds(par * 64 + t, 32, stride=2), :] = tile[k * 32:(k + 1) * 32]
    whole = jnp.sum(squares).reshape(1, 1)
    first = whole.astype(BF16).astype(F32)
    second = (whole - first).astype(BF16).astype(F32)
    third = whole - first - second
    lane = iota((DOM, LANES), 1)
    notes = jnp.broadcast_to(info[...], (DOM, LANES))
    parts = jnp.where(lane == 64, first, jnp.where(lane == 65, second, jnp.where(lane == 66, third, 0.0)))
    for k, extra in enumerate((pltpu.roll(notes, 64, 1), notes, parts)):
        at = pl.ds(1, DOM, stride=2)
        message[k, at, :] = jnp.where(lane < 64, message[k, at, :], extra)
    out[...] = packed(message)


def packed(message):
    whole = jnp.concatenate([message[k] for k in range(3)], axis=1)
    return whole.reshape(DOM, 2, 384).astype(BF16)


def unpacked(received, wide):
    whole = received[...].astype(F32).reshape(2 * DOM, 384)
    for k in range(3):
        wide[k] = whole[:, k * LANES:(k + 1) * LANES]


def permute_kernel(received, out, notes, squares, wide, message):
    unpacked(received, wide)
    odd = pl.ds(1, DOM, stride=2)
    info = wide[1, odd, :]
    notes[...] = pltpu.roll(wide[0, odd, :], 64, 1)
    upper = iota((DOM, LANES), 1) >= 64
    squares[...] = jnp.broadcast_to(
        jnp.sum(jnp.where(upper, wide[2, odd, :], 0.0)).reshape(1, 1), (1, LANES))
    rows = jnp.concatenate(
        [wide[k, pl.ds(t, DOM, stride=2), :].astype(BF16) for k in range(3) for t in range(2)], axis=1)
    lane = iota((DOM, LANES), 1)
    source = iota((DOM, DOM), 1).astype(F32)
    place = (iota((DOM, 256), 1) // CASES).astype(F32)
    chosen, keep = [], []
    for i in range(P_SIZE):
        device = jnp.sum(jnp.where(lane == 64 + i, info, 0.0), axis=1, keepdims=True)
        row = jnp.sum(jnp.where(lane == 76 + i, info, 0.0), axis=1, keepdims=True)
        chosen.append(one_hot(device == source))
        keep.append(row == place)
    taken = dot(jnp.concatenate(chosen, axis=0), rows)
    fold = one_hot(iota((256, LANES), 0) % CASES == iota((256, LANES), 1) % CASES)
    for k in range(3):
        kept = jnp.concatenate(
            [jnp.where(keep[i], taken[i * DOM:(i + 1) * DOM, k * 256:(k + 1) * 256], 0.0).astype(BF16)
             for i in range(P_SIZE)], axis=0)
        copies = dot(kept, fold)
        for t, count in ((0, LEAF), (1, ANC)):
            moved = jnp.zeros((DOM, LANES), F32)
            for i in range(count):
                at = (LEAF * t + i) * DOM
                moved = jnp.where(lane // CASES == i, copies[at:at + DOM], moved)
            message[k, pl.ds(t, DOM, stride=2), :] = moved
    out[...] = packed(message)


def left(ref, start, count):
    return jnp.concatenate(
        [ref[pl.ds(start, count), t].reshape(count * 8, LANES) for t in range(3)], axis=1)


def fetch_kernel(notes, inverses, tiles, out, ready, gather, near, sems):
    copies = [pltpu.make_async_copy(tiles.at[pl.ds(n * PAIRS, PAIRS)], near.at[pl.ds(n * PAIRS, PAIRS)],
                                    sems.at[n]) for n in range(LEAF // 2)]
    for copy in copies:
        copy.start()
    ready[...] = left(inverses, 0, PAIRS)
    gather[...] = one_hot(iota((B, 768), 1) // 8 == iota((B, 768), 0) // 2)
    for n, copy in enumerate(copies):
        copy.wait()
        out[:, n * 384:(n + 1) * 384] = left(near, n * PAIRS, PAIRS)


def select_kernel(targets, out):
    out[...] = one_hot(targets[...] == iota((256, 512), 0).astype(F32))


def update_kernel(received, ready, gather, tiles, early, level, ancestors, out,
                  wide, leaf, rest, right, near, sems, partial):
    copies = [pltpu.make_async_copy(tiles.at[pl.ds(k * PAIRS, PAIRS)], near.at[pl.ds((k - LEAF // 2) * PAIRS, PAIRS)],
                                    sems.at[k - LEAF // 2]) for k in range(LEAF // 2, LEAF)]
    for copy in copies:
        copy.start()
    unpacked(received, wide)
    for k in range(3):
        for par in range(2):
            at = pl.ds(2 * k + par, 32, stride=6)
            leaf[at, :] = wide[k, pl.ds(par * 64, 32, stride=2), :]
            rest[at, :] = wide[k, pl.ds(par * 64 + 1, 32, stride=2), :]

    def doubled(x):
        zeros = jnp.zeros_like(x)
        return jnp.concatenate(
            [jnp.concatenate([x, zeros], axis=1), jnp.concatenate([zeros, x], axis=1)], axis=0)

    solved = dot(ready[...], doubled(leaf[...].astype(BF16)))
    own = iota((768, 256), 0) % 8 == (iota((768, 256), 1) % LANES) // 16
    solved = jnp.where(own, solved, 0.0).astype(BF16)
    solved = dot(gather[...], solved)
    solved = jnp.where(iota((B, LANES), 0) % 2 == 0, solved[:, :LANES], solved[:, LANES:])
    unit = one_hot(iota((LANES, LANES), 0) == iota((LANES, LANES), 1))
    level[...] = lax.dot_general(unit, solved.astype(BF16), NT, preferred_element_type=F32).astype(BF16)
    ancestors[...] = lax.dot_general(
        unit[:64], rest[...].astype(BF16), NT, preferred_element_type=F32)
    owner = iota((B, LANES), 1) // 16
    for k in range(LEAF):
        right[k * 384:(k + 1) * 384] = doubled(jnp.where(owner == k, solved, 0.0)).astype(BF16)
    step, band = LEAF // 2, PAIRS // 2
    for first in range(0, LEAF, step):
        if first:
            for copy in copies:
                copy.wait()
        for r in range(0, PAIRS, band):
            at = slice(r * 8, (r + band) * 8)
            if first:
                wide_left = jnp.concatenate([left(near, k * PAIRS + r, band) for k in range(step)], axis=1)
            else:
                wide_left = early[at]
            total = dot(wide_left, right[first * 384:(first + step) * 384])
            if first == 0:
                partial[at] = total
            else:
                out[at] = (partial[at] + total).astype(BF16)


def sum_kernel(received, select, squares, out, squares_out, right):
    squares_out[...] = squares[...]
    group = iota((64, LANES), 1) // CASES
    for tile in range(3):
        parts = []
        for pair in range(tile * 4, tile * 4 + 4):
            rows = jnp.concatenate(
                [received[s, pair * 8:(pair + 1) * 8, :].astype(F32) for s in range(GROUP)], axis=0)
            parts.extend([rows[:, :LANES], rows[:, LANES:]])
        for step in (4, 2, 1):
            upper = (group // step) % 2 == 1
            turned = list(parts)
            for i in range(8):
                if not i & step:
                    a, b = parts[i], parts[i + step]
                    turned[i] = jnp.where(upper, pltpu.roll(b, step * CASES, 1), a)
                    turned[i + step] = jnp.where(upper, b, pltpu.roll(a, LANES - step * CASES, 1))
            parts = turned
        for k in range(LEAF):
            right[k * 64:(k + 1) * 64, tile * LANES:(tile + 1) * LANES] = parts[k].astype(BF16)
    out[...] = dot(select[...], right[...]).reshape(DOM, ANC, 384).astype(BF16)


def final_kernel(received, ancestors, out):
    place = iota((32, 256), 1)
    source, block = place // ANC, place % ANC
    group = source // (N_Z * N_CORE) * N_CORE + source % N_CORE
    row = iota((32, 256), 0)
    pick = one_hot((row % ANC == block) & (row // ANC == group))
    summed = dot(pick, received[...])
    count = ANC * CASES
    own = iota((count, 384), 1) % CASES == iota((count, 384), 0) % CASES
    sides = ([], [])
    for q in range(GROUP):
        left = jnp.concatenate(
            [jnp.broadcast_to(summed[q * ANC + t:q * ANC + t + 1], (CASES, 384)) for t in range(ANC)], axis=0)
        for side, part in zip(sides, halves(jnp.where(own, left, 0.0))):
            side.append(part)
    column = one_hot(iota((384, 24), 1) == iota((384, 24), 0) // CASES)
    both = dot(jnp.concatenate(sides[0] + sides[1], axis=0), column)
    both = both[:GROUP * count] + both[GROUP * count:]
    out[...] = ancestors[...] - jnp.concatenate(
        [both[q * count:(q + 1) * count] for q in range(GROUP)], axis=1)


def call(kernel, name, shapes, in_specs, scratch, megabytes=16, cost=None):
    outs = [jax.ShapeDtypeStruct(*s) for s in shapes]
    return pl.pallas_call(
        kernel,
        out_shape=outs,
        in_specs=in_specs,
        out_specs=[pl.BlockSpec(memory_space=pltpu.VMEM)] * len(outs),
        scratch_shapes=scratch,
        compiler_params=pltpu.CompilerParams(vmem_limit_bytes=megabytes * 2**20),
        cost_estimate=cost,
        name=name,
    )


def on_device(solution, loads, blocks, columns, row_source, inverses, tiles, targets):
    vmem = pl.BlockSpec(memory_space=pltpu.VMEM)
    smem = pl.BlockSpec(memory_space=pltpu.SMEM)
    hbm = pl.BlockSpec(memory_space=pltpu.HBM)
    dma = pltpu.SemaphoreType.DMA
    device = lax.axis_index("dom")
    far = lax.ppermute(solution, "dom", [(i, i + 1 if i % 2 else i - 1) for i in range(1, DOM - 1)])
    chip = lax.ppermute(solution, "dom", [(i, i ^ 1) for i in range(DOM)])
    local = columns.T - (device * P_SIZE - P_SIZE)
    turn = jnp.where(local < P_SIZE, 2 * P_SIZE, jnp.where(local < 2 * P_SIZE, 0, -2 * P_SIZE))
    local = local + jnp.where(device % 2 == 0, turn, 0)
    table = jnp.concatenate([
        jnp.pad(local, ((0, 0), (0, LANES - P_SIZE))),
        jnp.pad(row_source.reshape(1, P_SIZE), ((0, 3), (0, LANES - P_SIZE))),
        jnp.pad(targets, ((0, 0), (0, LANES - UPD)))], axis=0)
    natural = blocks.reshape(P_SIZE, NNZ, 288, LANES).transpose(0, 2, 1, 3).reshape(P_SIZE * 1152, LANES)
    natural_inverses = inverses.reshape(LEAF, 288, LANES).transpose(1, 0, 2).reshape(PAIRS, 3, LEAF, LANES)
    natural_tiles = tiles.reshape(LEAF, UPD, 288, LANES).transpose(0, 2, 1, 3)
    natural_tiles = natural_tiles.reshape(LEAF * PAIRS, 3, UPD, LANES)
    (lanes,) = call(
        lane_kernel, "lanes", [((ROWS, LANES), jnp.int32)], [], [], 16,
        pl.CostEstimate(flops=3 * 10**10, bytes_accessed=10**6, transcendentals=0))()
    high, low, cells, start, info = call(
        split_kernel, "split",
        [((P_SIZE, PAIRS, 1536), BF16), ((P_SIZE, PAIRS, 1536), BF16), ((2 * P_SIZE, 64, 384), BF16),
         ((P_SIZE, PAIRS, 64), F32), ((1, LANES), F32)],
        [smem, hbm] + [vmem] * 4,
        [pltpu.VMEM((P_SIZE, 64, 384), BF16), pltpu.VMEM((P_SIZE * 1152, LANES), F32), dma((P_SIZE,))], 41,
        pl.CostEstimate(flops=10**9, bytes_accessed=14 * 10**6, transcendentals=0),
    )(table, natural, chip, solution, loads, lanes)
    (message,) = call(
        residual_kernel, "residual", [((DOM, 2, 384), BF16)],
        [smem] + [vmem] * 6,
        [pltpu.VMEM((3 * P_SIZE, 64, 384), BF16), pltpu.VMEM((3, 2 * DOM, LANES), F32)], 16,
    )(table, high, low, cells, start, info, far)

    def exchange(x):
        return lax.all_to_all(x, "dom", 0, 0, tiled=True)

    def across(x, step):
        return x + lax.ppermute(x, "rhs", [(i, i ^ step) for i in range(4)])

    message, notes, squares = call(
        permute_kernel, "permute",
        [((DOM, 2, 384), BF16), ((DOM, LANES), F32), ((1, LANES), F32)], [vmem],
        [pltpu.VMEM((3, 2 * DOM, LANES), F32), pltpu.VMEM((3, 2 * DOM, LANES), F32)], 16,
        pl.CostEstimate(flops=4 * 10**9, bytes_accessed=10**6, transcendentals=0),
    )(exchange(message))

    half = (LEAF // 2 * PAIRS, 3, UPD, LANES)
    early, ready, gather = call(
        fetch_kernel, "fetch",
        [((PAIRS * UPD, LEAF // 2 * 384), BF16), ((PAIRS * LEAF, 384), BF16), ((B, PAIRS * LEAF), BF16)],
        [vmem, vmem, hbm], [pltpu.VMEM(half, BF16), dma((LEAF // 2,))], 50,
        pl.CostEstimate(flops=2 * 10**9, bytes_accessed=10**6, transcendentals=0),
    )(notes, natural_inverses, natural_tiles)
    level, ancestors, message = call(
        update_kernel, "update",
        [((LEAF * CASES, B), BF16), ((ANC * CASES, B), F32), ((PAIRS * UPD, 256), BF16)],
        [vmem, vmem, vmem, hbm, vmem],
        [pltpu.VMEM((3, 2 * DOM, LANES), F32), pltpu.VMEM((B, LANES), F32), pltpu.VMEM((B, LANES), F32),
         pltpu.VMEM((LEAF * 384, 256), BF16), pltpu.VMEM(half, BF16),
         dma((LEAF // 2,)), pltpu.VMEM((PAIRS * UPD, 256), F32)], 48,
    )(exchange(message), ready, gather, natural_tiles, early)

    groups = [[(x * N_Z + z) * N_CORE + c for x in range(N_X) for c in range(N_CORE)] for z in range(N_Z)]
    received = lax.all_to_all(
        message.reshape(GROUP, 96, 256), "dom", 0, 0, axis_index_groups=groups, tiled=True)
    z = (device // N_CORE) % N_Z
    near = lax.dynamic_index_in_dim(notes.reshape(N_X, N_Z, N_CORE, LANES), z, axis=1, keepdims=False)
    near = near.reshape(GROUP, LANES)[:, :LEAF * UPD].reshape(GROUP, LEAF, UPD)
    near = near.transpose(1, 0, 2).reshape(1, LEAF * GROUP * UPD)
    (select,) = call(select_kernel, "select", [((256, 512), BF16)], [vmem], [], 16,
                     pl.CostEstimate(flops=10**9, bytes_accessed=10**6, transcendentals=0))(near)
    sums, squares = call(
        sum_kernel, "sum", [((DOM, ANC, 384), BF16), ((1, LANES), F32)], [vmem] * 3,
        [pltpu.VMEM((512, 384), BF16)],
    )(received, select, across(squares, 1))
    residual_rms = jnp.sqrt(across(squares, 2)[0, 0] / (DOM * P_SIZE * CASES * 4 * B))
    sums = lax.all_to_all(sums, "dom", 0, 0, tiled=True)
    (ancestor_rhs,) = call(final_kernel, "final", [((ANC * CASES, B), F32)], [vmem] * 2, [])(
        sums.reshape(DOM * ANC, 384), ancestors)
    return (level.reshape(LEAF, CASES, B), ancestor_rhs.reshape(ANC, CASES, B), residual_rms)


def solution(mesh):
    placed = (
        P("dom", "rhs", None),
        P("dom", "rhs", None),
        P("dom", None, None),
        P("dom", None),
        P("dom"),
        P("dom", None),
        P("dom", None, None),
        P("dom", None),
    )
    return jax.shard_map(
        on_device,
        mesh=mesh,
        in_specs=placed,
        out_specs=(P("dom", "rhs", None), P("dom", "rhs", None), P()),
        check_vma=False,
    )
```

```python
import jax
import jax.numpy as jnp
from jax import lax
from jax.experimental import pallas as pl
from jax.experimental.pallas import tpu as pltpu
from jax.sharding import PartitionSpec as P

B = 192
LEAF = 8
ANC = 4
NNZ = 4
UPD = 8
P_SIZE = 12
CASES = 16
DOM = 64
N_X, N_Z, N_CORE = 4, 8, 2
GROUP = N_X * N_CORE
LANES = 128
ROWS = 8
PAIRS = B // 2
BF16 = jnp.bfloat16
F32 = jnp.float32
NT = (((1,), (1,)), ((), ()))


def iota(shape, dim):
    return lax.broadcasted_iota(jnp.int32, shape, dim)


def one_hot(condition):
    return jnp.where(condition, 1.0, 0.0).astype(BF16)


def halves(x):
    high = x.astype(BF16)
    return high, (x - high.astype(F32)).astype(BF16)


def dot(a, b):
    return jnp.dot(a, b, preferred_element_type=F32)


def put_cells(x, cells, slot):
    wide, narrow = x[:, :LANES], jnp.concatenate([x[:, LANES:], jnp.zeros((CASES, 64), F32)], axis=1)
    lower = iota((CASES, LANES), 1) < 64
    zeros = jnp.zeros((CASES, LANES), F32)
    turned = pltpu.roll(wide, 64, 1)
    lines = (
        (wide, narrow, zeros),
        (zeros, jnp.where(lower, 0.0, turned), jnp.where(lower, turned, pltpu.roll(narrow, 64, 1))),
    )
    for par in range(2):
        for t in range(3):
            for part, value in enumerate(halves(lines[par][t])):
                row = (2 * par + part) * CASES
                cells[slot, row:row + CASES, t * LANES:(t + 1) * LANES] = value


def lane_kernel(out):
    out[...] = iota((ROWS, LANES), 1)


def split_kernel(table, blocks, chip, own, loads, lanes, high, low, cells, start, info,
                 load_cells, wide, sems):
    count = NNZ * 288
    copies = [pltpu.make_async_copy(blocks.at[pl.ds(g * count, count)], wide.at[pl.ds(g * count, count)],
                                    sems.at[g]) for g in range(P_SIZE)]
    for copy in copies:
        copy.start()
    for i in range(P_SIZE):
        put_cells(loads[i], load_cells, i)
        put_cells(chip[i], cells, i)
        put_cells(own[i], cells, P_SIZE + i)
    unit_row, unit_col = iota((PAIRS, 384), 0), iota((PAIRS, 384), 1)
    pair = (unit_row % 32) * 3 + unit_row // 32
    unit = one_hot((unit_col == 2 * pair) | (unit_col == 2 * pair + B + 1))
    for g in range(P_SIZE):
        start[g] = lax.dot_general(unit, load_cells[g], NT, preferred_element_type=F32)
    lane = lanes[...]
    notes = jnp.zeros((ROWS, LANES), jnp.int32)
    for k in range(LEAF):
        for m in range(UPD):
            notes = jnp.where(lane == k * UPD + m, table[8 + k, m], notes)
    for i in range(P_SIZE):
        source = table[4, i]
        notes = jnp.where(lane == 64 + i, source // P_SIZE, notes)
        notes = jnp.where(lane == 76 + i, source % P_SIZE, notes)
    info[...] = notes.astype(F32)[:1]

    for g in range(P_SIZE):
        if g % 2 == 0:
            for copy in copies[g:g + 2]:
                copy.wait()
        for j in range(NNZ):
            for t in range(3):
                tall = jnp.concatenate(
                    [wide[pl.ds(g * count + 12 * k + j + 4 * t, 32, stride=36), :] for k in range(3)], axis=0)
                at = (g, slice(None), slice(j * 384 + t * LANES, j * 384 + (t + 1) * LANES))
                high[at], low[at] = halves(tall)


def residual_kernel(table, high, low, near, start, info, far, out, cells, message):
    for i in range(P_SIZE):
        cells[i] = near[i]
        cells[P_SIZE + i] = near[P_SIZE + i]
        put_cells(far[i], cells, 2 * P_SIZE + i)

    residuals = ([], [])
    for g in range(P_SIZE):
        right = jnp.concatenate([cells[table[j, g]] for j in range(NNZ)], axis=1)
        total = start[g]
        for side in (high, low):
            total = total - lax.dot_general(side[g], right, NT, preferred_element_type=F32)
        for par in range(2):
            one = total[:, par * 32:par * 32 + 16] + total[:, par * 32 + 16:par * 32 + 32]
            residuals[par].append(one)

    squares = jnp.zeros((PAIRS, LANES), F32)
    for par in range(2):
        ones = residuals[par] + [jnp.zeros((PAIRS, CASES), F32)] * 4
        for t in range(2):
            tile = jnp.concatenate(ones[8 * t:8 * t + 8], axis=1)
            squares = squares + tile * tile
            for k in range(3):
                message[k, pl.ds(par * 64 + t, 32, stride=2), :] = tile[k * 32:(k + 1) * 32]
    whole = jnp.sum(squares).reshape(1, 1)
    first = whole.astype(BF16).astype(F32)
    second = (whole - first).astype(BF16).astype(F32)
    third = whole - first - second
    lane = iota((DOM, LANES), 1)
    notes = jnp.broadcast_to(info[...], (DOM, LANES))
    parts = jnp.where(lane == 64, first, jnp.where(lane == 65, second, jnp.where(lane == 66, third, 0.0)))
    for k, extra in enumerate((pltpu.roll(notes, 64, 1), notes, parts)):
        at = pl.ds(1, DOM, stride=2)
        message[k, at, :] = jnp.where(lane < 64, message[k, at, :], extra)
    out[...] = packed(message)


def packed(message):
    whole = jnp.concatenate([message[k] for k in range(3)], axis=1)
    return whole.reshape(DOM, 2, 384).astype(BF16)


def unpacked(received, wide):
    whole = received[...].astype(F32).reshape(2 * DOM, 384)
    for k in range(3):
        wide[k] = whole[:, k * LANES:(k + 1) * LANES]


def permute_kernel(received, out, notes, squares, wide, message):
    unpacked(received, wide)
    odd = pl.ds(1, DOM, stride=2)
    info = wide[1, odd, :]
    notes[...] = pltpu.roll(wide[0, odd, :], 64, 1)
    upper = iota((DOM, LANES), 1) >= 64
    squares[...] = jnp.broadcast_to(
        jnp.sum(jnp.where(upper, wide[2, odd, :], 0.0)).reshape(1, 1), (1, LANES))
    rows = jnp.concatenate(
        [wide[k, pl.ds(t, DOM, stride=2), :].astype(BF16) for k in range(3) for t in range(2)], axis=1)
    lane = iota((DOM, LANES), 1)
    source = iota((DOM, DOM), 1).astype(F32)
    place = (iota((DOM, 256), 1) // CASES).astype(F32)
    chosen, keep = [], []
    for i in range(P_SIZE):
        device = jnp.sum(jnp.where(lane == 64 + i, info, 0.0), axis=1, keepdims=True)
        row = jnp.sum(jnp.where(lane == 76 + i, info, 0.0), axis=1, keepdims=True)
        chosen.append(one_hot(device == source))
        keep.append(row == place)
    taken = dot(jnp.concatenate(chosen, axis=0), rows)
    fold = one_hot(iota((256, LANES), 0) % CASES == iota((256, LANES), 1) % CASES)
    for k in range(3):
        kept = jnp.concatenate(
            [jnp.where(keep[i], taken[i * DOM:(i + 1) * DOM, k * 256:(k + 1) * 256], 0.0).astype(BF16)
             for i in range(P_SIZE)], axis=0)
        copies = dot(kept, fold)
        for t, count in ((0, LEAF), (1, ANC)):
            moved = jnp.zeros((DOM, LANES), F32)
            for i in range(count):
                at = (LEAF * t + i) * DOM
                moved = jnp.where(lane // CASES == i, copies[at:at + DOM], moved)
            message[k, pl.ds(t, DOM, stride=2), :] = moved
    out[...] = packed(message)


def left(ref, start, count):
    return jnp.concatenate(
        [ref[pl.ds(start, count), t].reshape(count * 8, LANES) for t in range(3)], axis=1)


def fetch_kernel(notes, inverses, tiles, out, ready, gather, near, sems):
    copies = [pltpu.make_async_copy(tiles.at[pl.ds(n * PAIRS, PAIRS)], near.at[pl.ds(n * PAIRS, PAIRS)],
                                    sems.at[n]) for n in range(LEAF // 2)]
    for copy in copies:
        copy.start()
    ready[...] = left(inverses, 0, PAIRS)
    gather[...] = one_hot(iota((B, 768), 1) // 8 == iota((B, 768), 0) // 2)
    for n, copy in enumerate(copies):
        copy.wait()
        out[:, n * 384:(n + 1) * 384] = left(near, n * PAIRS, PAIRS)


def select_kernel(targets, out):
    out[...] = one_hot(targets[...] == iota((256, 512), 0).astype(F32))


def turn_kernel(solved, rest, level, ancestors):
    unit = one_hot(iota((LANES, LANES), 0) == iota((LANES, LANES), 1))
    level[...] = lax.dot_general(unit, solved[...], NT, preferred_element_type=F32).astype(BF16)
    ancestors[...] = lax.dot_general(
        unit[:64], rest[...].astype(BF16), NT, preferred_element_type=F32)


def update_kernel(received, ready, gather, tiles, early, level, rest, out,
                  wide, leaf, right, near, sems, partial):
    copies = [pltpu.make_async_copy(tiles.at[pl.ds(k * PAIRS, PAIRS)], near.at[pl.ds((k - LEAF // 2) * PAIRS, PAIRS)],
                                    sems.at[k - LEAF // 2]) for k in range(LEAF // 2, LEAF)]
    for copy in copies:
        copy.start()
    unpacked(received, wide)
    for k in range(3):
        for par in range(2):
            at = pl.ds(2 * k + par, 32, stride=6)
            leaf[at, :] = wide[k, pl.ds(par * 64, 32, stride=2), :]
            rest[at, :] = wide[k, pl.ds(par * 64 + 1, 32, stride=2), :]

    def doubled(x):
        zeros = jnp.zeros_like(x)
        return jnp.concatenate(
            [jnp.concatenate([x, zeros], axis=1), jnp.concatenate([zeros, x], axis=1)], axis=0)

    solved = dot(ready[...], doubled(leaf[...].astype(BF16)))
    own = iota((768, 256), 0) % 8 == (iota((768, 256), 1) % LANES) // 16
    solved = jnp.where(own, solved, 0.0).astype(BF16)
    solved = dot(gather[...], solved)
    solved = jnp.where(iota((B, LANES), 0) % 2 == 0, solved[:, :LANES], solved[:, LANES:])
    level[...] = solved.astype(BF16)
    owner = iota((B, LANES), 1) // 16
    for k in range(LEAF):
        right[k * 384:(k + 1) * 384] = doubled(jnp.where(owner == k, solved, 0.0)).astype(BF16)
    step, band = LEAF // 2, PAIRS // 2
    for first in range(0, LEAF, step):
        if first:
            for copy in copies:
                copy.wait()
        for r in range(0, PAIRS, band):
            at = slice(r * 8, (r + band) * 8)
            if first:
                wide_left = jnp.concatenate([left(near, k * PAIRS + r, band) for k in range(step)], axis=1)
            else:
                wide_left = early[at]
            total = dot(wide_left, right[first * 384:(first + step) * 384])
            if first == 0:
                partial[at] = total
            else:
                out[at] = (partial[at] + total).astype(BF16)


def sum_kernel(received, select, squares, out, squares_out, right):
    squares_out[...] = squares[...]
    group = iota((64, LANES), 1) // CASES
    for tile in range(3):
        parts = []
        for pair in range(tile * 4, tile * 4 + 4):
            rows = jnp.concatenate(
                [received[s, pair * 8:(pair + 1) * 8, :].astype(F32) for s in range(GROUP)], axis=0)
            parts.extend([rows[:, :LANES], rows[:, LANES:]])
        for step in (4, 2, 1):
            upper = (group // step) % 2 == 1
            turned = list(parts)
            for i in range(8):
                if not i & step:
                    a, b = parts[i], parts[i + step]
                    turned[i] = jnp.where(upper, pltpu.roll(b, step * CASES, 1), a)
                    turned[i + step] = jnp.where(upper, b, pltpu.roll(a, LANES - step * CASES, 1))
            parts = turned
        for k in range(LEAF):
            right[k * 64:(k + 1) * 64, tile * LANES:(tile + 1) * LANES] = parts[k].astype(BF16)
    out[...] = dot(select[...], right[...]).reshape(DOM, ANC, 384).astype(BF16)


def final_kernel(received, ancestors, out):
    place = iota((32, 256), 1)
    source, block = place // ANC, place % ANC
    group = source // (N_Z * N_CORE) * N_CORE + source % N_CORE
    row = iota((32, 256), 0)
    pick = one_hot((row % ANC == block) & (row // ANC == group))
    summed = dot(pick, received[...])
    count = ANC * CASES
    own = iota((count, 384), 1) % CASES == iota((count, 384), 0) % CASES
    sides = ([], [])
    for q in range(GROUP):
        left = jnp.concatenate(
            [jnp.broadcast_to(summed[q * ANC + t:q * ANC + t + 1], (CASES, 384)) for t in range(ANC)], axis=0)
        for side, part in zip(sides, halves(jnp.where(own, left, 0.0))):
            side.append(part)
    column = one_hot(iota((384, 24), 1) == iota((384, 24), 0) // CASES)
    both = dot(jnp.concatenate(sides[0] + sides[1], axis=0), column)
    both = both[:GROUP * count] + both[GROUP * count:]
    out[...] = ancestors[...] - jnp.concatenate(
        [both[q * count:(q + 1) * count] for q in range(GROUP)], axis=1)


def call(kernel, name, shapes, in_specs, scratch, megabytes=16, cost=None):
    outs = [jax.ShapeDtypeStruct(*s) for s in shapes]
    return pl.pallas_call(
        kernel,
        out_shape=outs,
        in_specs=in_specs,
        out_specs=[pl.BlockSpec(memory_space=pltpu.VMEM)] * len(outs),
        scratch_shapes=scratch,
        compiler_params=pltpu.CompilerParams(vmem_limit_bytes=megabytes * 2**20),
        cost_estimate=cost,
        name=name,
    )


def on_device(solution, loads, blocks, columns, row_source, inverses, tiles, targets):
    vmem = pl.BlockSpec(memory_space=pltpu.VMEM)
    smem = pl.BlockSpec(memory_space=pltpu.SMEM)
    hbm = pl.BlockSpec(memory_space=pltpu.HBM)
    dma = pltpu.SemaphoreType.DMA
    device = lax.axis_index("dom")
    far = lax.ppermute(solution, "dom", [(i, i + 1 if i % 2 else i - 1) for i in range(1, DOM - 1)])
    chip = lax.ppermute(solution, "dom", [(i, i ^ 1) for i in range(DOM)])
    local = columns.T - (device * P_SIZE - P_SIZE)
    turn = jnp.where(local < P_SIZE, 2 * P_SIZE, jnp.where(local < 2 * P_SIZE, 0, -2 * P_SIZE))
    local = local + jnp.where(device % 2 == 0, turn, 0)
    table = jnp.concatenate([
        jnp.pad(local, ((0, 0), (0, LANES - P_SIZE))),
        jnp.pad(row_source.reshape(1, P_SIZE), ((0, 3), (0, LANES - P_SIZE))),
        jnp.pad(targets, ((0, 0), (0, LANES - UPD)))], axis=0)
    natural = blocks.reshape(P_SIZE, NNZ, 288, LANES).transpose(0, 2, 1, 3).reshape(P_SIZE * 1152, LANES)
    natural_inverses = inverses.reshape(LEAF, 288, LANES).transpose(1, 0, 2).reshape(PAIRS, 3, LEAF, LANES)
    natural_tiles = tiles.reshape(LEAF, UPD, 288, LANES).transpose(0, 2, 1, 3)
    natural_tiles = natural_tiles.reshape(LEAF * PAIRS, 3, UPD, LANES)
    (lanes,) = call(
        lane_kernel, "lanes", [((ROWS, LANES), jnp.int32)], [], [], 16,
        pl.CostEstimate(flops=3 * 10**10, bytes_accessed=10**6, transcendentals=0))()
    high, low, cells, start, info = call(
        split_kernel, "split",
        [((P_SIZE, PAIRS, 1536), BF16), ((P_SIZE, PAIRS, 1536), BF16), ((2 * P_SIZE, 64, 384), BF16),
         ((P_SIZE, PAIRS, 64), F32), ((1, LANES), F32)],
        [smem, hbm] + [vmem] * 4,
        [pltpu.VMEM((P_SIZE, 64, 384), BF16), pltpu.VMEM((P_SIZE * 1152, LANES), F32), dma((P_SIZE,))], 41,
        pl.CostEstimate(flops=10**9, bytes_accessed=14 * 10**6, transcendentals=0),
    )(table, natural, chip, solution, loads, lanes)
    (message,) = call(
        residual_kernel, "residual", [((DOM, 2, 384), BF16)],
        [smem] + [vmem] * 6,
        [pltpu.VMEM((3 * P_SIZE, 64, 384), BF16), pltpu.VMEM((3, 2 * DOM, LANES), F32)], 16,
    )(table, high, low, cells, start, info, far)

    def exchange(x):
        return lax.all_to_all(x, "dom", 0, 0, tiled=True)

    def across(x, step):
        return x + lax.ppermute(x, "rhs", [(i, i ^ step) for i in range(4)])

    message, notes, squares = call(
        permute_kernel, "permute",
        [((DOM, 2, 384), BF16), ((DOM, LANES), F32), ((1, LANES), F32)], [vmem],
        [pltpu.VMEM((3, 2 * DOM, LANES), F32), pltpu.VMEM((3, 2 * DOM, LANES), F32)], 16,
        pl.CostEstimate(flops=4 * 10**9, bytes_accessed=10**6, transcendentals=0),
    )(exchange(message))

    half = (LEAF // 2 * PAIRS, 3, UPD, LANES)
    early, ready, gather = call(
        fetch_kernel, "fetch",
        [((PAIRS * UPD, LEAF // 2 * 384), BF16), ((PAIRS * LEAF, 384), BF16), ((B, PAIRS * LEAF), BF16)],
        [vmem, vmem, hbm], [pltpu.VMEM(half, BF16), dma((LEAF // 2,))], 50,
        pl.CostEstimate(flops=2 * 10**9, bytes_accessed=10**6, transcendentals=0),
    )(notes, natural_inverses, natural_tiles)
    solved, rest, message = call(
        update_kernel, "update",
        [((B, LANES), BF16), ((B, LANES), F32), ((PAIRS * UPD, 256), BF16)],
        [vmem, vmem, vmem, hbm, vmem],
        [pltpu.VMEM((3, 2 * DOM, LANES), F32), pltpu.VMEM((B, LANES), F32),
         pltpu.VMEM((LEAF * 384, 256), BF16), pltpu.VMEM(half, BF16),
         dma((LEAF // 2,)), pltpu.VMEM((PAIRS * UPD, 256), F32)], 48,
    )(exchange(message), ready, gather, natural_tiles, early)

    level, ancestors = call(
        turn_kernel, "turn", [((LEAF * CASES, B), BF16), ((ANC * CASES, B), F32)], [vmem] * 2, [], 16,
        pl.CostEstimate(flops=10**9, bytes_accessed=10**6, transcendentals=0))(solved, rest)
    groups = [[(x * N_Z + z) * N_CORE + c for x in range(N_X) for c in range(N_CORE)] for z in range(N_Z)]
    received = lax.all_to_all(
        message.reshape(GROUP, 96, 256), "dom", 0, 0, axis_index_groups=groups, tiled=True)
    z = (device // N_CORE) % N_Z
    near = lax.dynamic_index_in_dim(notes.reshape(N_X, N_Z, N_CORE, LANES), z, axis=1, keepdims=False)
    near = near.reshape(GROUP, LANES)[:, :LEAF * UPD].reshape(GROUP, LEAF, UPD)
    near = near.transpose(1, 0, 2).reshape(1, LEAF * GROUP * UPD)
    (select,) = call(select_kernel, "select", [((256, 512), BF16)], [vmem], [], 16,
                     pl.CostEstimate(flops=10**9, bytes_accessed=10**6, transcendentals=0))(near)
    sums, squares = call(
        sum_kernel, "sum", [((DOM, ANC, 384), BF16), ((1, LANES), F32)], [vmem] * 3,
        [pltpu.VMEM((512, 384), BF16)],
    )(received, select, across(squares, 1))
    residual_rms = jnp.sqrt(across(squares, 2)[0, 0] / (DOM * P_SIZE * CASES * 4 * B))
    sums = lax.all_to_all(sums, "dom", 0, 0, tiled=True)
    (ancestor_rhs,) = call(final_kernel, "final", [((ANC * CASES, B), F32)], [vmem] * 2, [])(
        sums.reshape(DOM * ANC, 384), ancestors)
    return (level.reshape(LEAF, CASES, B), ancestor_rhs.reshape(ANC, CASES, B), residual_rms)


def solution(mesh):
    placed = (
        P("dom", "rhs", None),
        P("dom", "rhs", None),
        P("dom", None, None),
        P("dom", None),
        P("dom"),
        P("dom", None),
        P("dom", None, None),
        P("dom", None),
    )
    return jax.shard_map(
        on_device,
        mesh=mesh,
        in_specs=placed,
        out_specs=(P("dom", "rhs", None), P("dom", "rhs", None), P()),
        check_vma=False,
    )
```
